512 devices in a mesh: wide: 128 (over z, x, core), narrow: 4 (over y).
Axes of the slice: x: 4, y: 4, z: 16, core: 2. Of those that a mesh axis runs over, the one named last changes fastest.
Arguments:
- features: bfloat16 [128, 4, 512, 128], P('wide', 'narrow'), may hold values from -6 to 6
- send_rows: int32 [128, 4, 128, 2], P('wide', 'narrow'), may hold values from 0 to 511
- send_counts: int32 [128, 4, 128], P('wide', 'narrow'), may hold values from 1 to 2, as said below
- tile_index: int32 [128, 4, 4, 3], P('wide', 'narrow'), may hold values from 0 to 5, as said below
- tile_weight: bfloat16 [128, 4, 4, 3, 128, 128], P('wide', 'narrow'), may hold values from -0.3125 to 0.3125
- first_layer_self_weight: bfloat16 [128, 256], replicated, may hold values from -0.5 to 0.5
- first_layer_neighbour_weight: bfloat16 [128, 256], replicated, may hold values from -0.5 to 0.5
- layer1_bias: float32 [256], replicated, may hold values from -3 to 3
- layer2_self: bfloat16 [256, 172], replicated, may hold values from -0.375 to 0.375
- layer2_neigh: bfloat16 [256, 172], replicated, may hold values from -0.375 to 0.375
- grad_logits: bfloat16 [128, 4, 512, 172], P('wide', 'narrow'), may hold values from -0.01171875 to 0.01171875
Outputs:
- logits: bfloat16 [128, 4, 512, 172], P('wide', 'narrow')
- first_self_weight_gradient: float32 [128, 256], replicated
- first_neighbour_weight_gradient: float32 [128, 256], replicated
- grad_bias1: float32 [256], replicated
- grad_self2: float32 [256, 172], replicated
- grad_neigh2: float32 [256, 172], replicated
The draws below stay inside these ranges and needn't reach their ends.
Inputs may be any that keep to these rules, and one draw needn't show every extreme that they name: `send_counts`: every sub-partition fills all 2 slots toward at least one peer. `tile_index`: indices count 128-row blocks of the extended rows (own rows, then received rows). Tile 0 of block b is the own block b; tile 1 is a received block, and every received block is read by some tile of the sub-partition.
All inputs are finite; a program needn't handle non-finite values.
Results may differ from the reference program's by a relative error of at most 0.015.
The reference program's roundings to bfloat16 on the way count: a program that leaves them out, or rounds other values in their place, can miss the bound.
Values may be sent and summed in bfloat16 or wider, within the bound.
No kernel may reach another device: no remote copies, remote signals or barrier semaphores. Data moves between devices by JAX's collectives and lax.ppermute only.
A program may use at most 64 MiB of HBM per device.

```python
import jax
import jax.numpy as jnp
from jax import lax

F_IN = 128
HID = 256
CLS = 172
ROWS_DEV = 512
RECV_BLOCKS = 2
TILES = 3
SLOT = 2
ROW_BLOCKS = 4
EXT_BLOCKS = 6
N_WIDE = 128
N_NARROW = 4


def draw_send_counts(key, part):
    key = jax.random.fold_in(key, 7)
    first_key, second_key = jax.random.split(key)
    counts = jax.random.randint(first_key, (N_WIDE, N_NARROW, N_WIDE), 1, SLOT + 1)
    full_peer = jax.random.randint(second_key, (N_WIDE, N_NARROW, 1), 0, N_WIDE)
    peers = jnp.arange(N_WIDE, dtype=jnp.int32)[None, None, :]
    return jnp.where(peers == full_peer, SLOT, counts).astype(jnp.int32)


def draw_tile_index(key, part):
    key = jax.random.fold_in(key, 11)
    first_key, second_key = jax.random.split(key)
    offset = jax.random.randint(first_key, (N_WIDE, N_NARROW, 1), 0, RECV_BLOCKS)
    positions = jnp.arange(ROW_BLOCKS, dtype=jnp.int32)[None, None, :]
    own_block = jnp.broadcast_to(positions, (N_WIDE, N_NARROW, ROW_BLOCKS))
    far_block = ROW_BLOCKS + (positions + offset) % RECV_BLOCKS
    others = jax.random.randint(second_key, (N_WIDE, N_NARROW, ROW_BLOCKS, TILES - 2), 0, EXT_BLOCKS)
    stacked = jnp.concatenate([own_block[..., None], far_block[..., None], others], axis=-1)
    return stacked.astype(jnp.int32)


def set_ends(array, stream_key, least, high):
    index_at = [jax.random.randint(jax.random.fold_in(stream_key, axis), (), 0, length) for axis, length in enumerate(array.shape)]
    widest = array.shape.index(max(array.shape))
    next_to = index_at[:widest] + [(index_at[widest] + 1) % array.shape[widest]] + index_at[widest + 1:]
    return array.at[tuple(index_at)].set(least).at[tuple(next_to)].set(high)


def level_of(key, extent, cuts, least, top_value):
    def one(position, blocks):
        draws = jax.random.uniform(jax.random.fold_in(jax.random.fold_in(key, 6), position), (blocks,), jnp.float32, least / len(cuts), top_value / len(cuts))
        return jnp.repeat(jnp.exp(draws), extent[position] // blocks).reshape((-1,) + (1,) * (len(extent) - position - 1))

    loudness = one(*cuts[0])
    for cut in cuts[1:]:
        loudness = loudness * one(*cut)
    return loudness


def gaussian(key, extent, spread, bound, cuts=(), held_as=jnp.bfloat16):
    entries = jax.random.normal(key, extent, jnp.float32) * spread
    if len(cuts) > 0:
        entries = level_of(key, extent, cuts, -0.22, 0.18) * entries
    return jnp.clip(entries, min=-bound, max=bound).astype(held_as)


def setup_inputs(seed: int = 0) -> dict:
    key_list = jax.random.split(jax.random.key(seed), 12)
    return {
        "features": gaussian(key_list[0], (N_WIDE, N_NARROW, ROWS_DEV, F_IN), 1.0, 6.0, ((0, 128), (1, 4))),
        "send_rows": set_ends(jax.random.randint(key_list[1], (N_WIDE, N_NARROW, N_WIDE, SLOT), 0, ROWS_DEV), jax.random.fold_in(key_list[1], 1), 0, ROWS_DEV - 1).astype(jnp.int32),
        "send_counts": draw_send_counts(jax.random.fold_in(key_list[11], 71), 0),
        "tile_index": draw_tile_index(jax.random.fold_in(key_list[11], 71), 0),
        "tile_weight": gaussian(key_list[4], (N_WIDE, N_NARROW, ROW_BLOCKS, TILES, 128, 128), (TILES * 128) ** -0.5, 0.3125, ((0, 128), (1, 4))),
        "first_layer_self_weight": gaussian(key_list[5], (F_IN, HID), F_IN ** -0.5, 0.5),
        "first_layer_neighbour_weight": gaussian(key_list[6], (F_IN, HID), F_IN ** -0.5, 0.5),
        "layer1_bias": gaussian(key_list[7], (HID,), 0.5, 3.0, (), jnp.float32),
        "layer2_self": gaussian(key_list[8], (HID, CLS), HID ** -0.5, 0.375),
        "layer2_neigh": gaussian(key_list[9], (HID, CLS), HID ** -0.5, 0.375),
        "grad_logits": gaussian(key_list[10], (N_WIDE, N_NARROW, ROWS_DEV, CLS), ((ROWS_DEV * N_WIDE * N_NARROW) ** -0.5), 0.01171875, ((0, 128), (1, 4))),
    }


def aggregate(tile_weight, tile_index, extended):
    columns = extended.shape[-1]
    blocks = extended.reshape(-1, 128, columns)
    picked = blocks[tile_index]
    summed = jnp.einsum("bkij,bkjf->bif", tile_weight.astype(jnp.float32), picked.astype(jnp.float32), precision=lax.Precision.HIGHEST)
    return summed.reshape(-1, columns)


def spread_back(tile_weight, tile_index, grads):
    columns = grads.shape[-1]
    row_blocks = tile_index.shape[0]
    shaped = grads.reshape(row_blocks, 128, columns)
    contrib = jnp.einsum("bkij,bif->bkjf", tile_weight.astype(grads.dtype), shaped, precision=lax.Precision.HIGHEST)
    onehot = (tile_index.reshape(-1)[:, None] == jnp.arange(EXT_BLOCKS, dtype=jnp.int32)[None, :]).astype(grads.dtype)
    flat = contrib.reshape(onehot.shape[0], -1)
    summed = jnp.dot(onehot.T, flat, precision=lax.Precision.HIGHEST)
    return summed.reshape(EXT_BLOCKS * 128, columns)


def pick_rows(table_one, rows_one):
    return table_one[rows_one]


def add_rows(rows_one, values):
    empty = jnp.zeros((ROWS_DEV, values.shape[-1]), values.dtype)
    return empty.at[rows_one].add(values)


def reference(features, send_rows, send_counts, tile_index, tile_weight, first_layer_self_weight, first_layer_neighbour_weight, layer1_bias, layer2_self, layer2_neigh, grad_logits):
    devices = N_WIDE * N_NARROW
    maximal_precision = lax.Precision.HIGHEST
    flattened_vertex_features = features.reshape(devices, ROWS_DEV, F_IN)
    flat_rows = send_rows.reshape(devices, N_WIDE * SLOT)
    live_slot = (jnp.arange(SLOT, dtype=jnp.int32)[None, None, None, :] < send_counts[..., None]).reshape(devices, N_WIDE * SLOT)
    flat_index = tile_index.reshape(devices, ROW_BLOCKS, TILES)
    flat_tiles = tile_weight.reshape(devices, ROW_BLOCKS, TILES, 128, 128)

    def extend(table):
        columns = table.shape[-1]
        picked = jax.vmap(pick_rows)(table, flat_rows)
        sent = jnp.where(live_slot[..., None], picked, jnp.zeros((), table.dtype))
        moved = sent.reshape(N_WIDE, N_NARROW, N_WIDE, SLOT, columns).transpose(2, 1, 0, 3, 4)
        return jnp.concatenate([table, moved.reshape(devices, N_WIDE * SLOT, columns)], axis=1)

    def one_device(items):
        return aggregate(items[0], items[1], items[2])

    def one_back(items):
        return spread_back(items[0], items[1], items[2])

    neighbour_feature_sum = lax.map(one_device, (flat_tiles, flat_index, extend(flattened_vertex_features))).astype(jnp.bfloat16)
    preactivation_values = jnp.einsum("vsj,jq->vsq", flattened_vertex_features.astype(jnp.float32), first_layer_self_weight.astype(jnp.float32), precision=maximal_precision)
    preactivation_values = preactivation_values + jnp.einsum("vsj,jq->vsq", neighbour_feature_sum.astype(jnp.float32), first_layer_neighbour_weight.astype(jnp.float32), precision=maximal_precision)
    preactivation_values = preactivation_values + layer1_bias
    hidden = jnp.maximum(preactivation_values, 0.0).astype(jnp.bfloat16)
    agg_hidden = lax.map(one_device, (flat_tiles, flat_index, extend(hidden))).astype(jnp.bfloat16)
    hidden_f = hidden.astype(jnp.float32)
    agg_hidden_f = agg_hidden.astype(jnp.float32)
    scores = jnp.einsum("drh,hc->drc", hidden_f, layer2_self.astype(jnp.float32), precision=maximal_precision)
    scores = scores + jnp.einsum("drh,hc->drc", agg_hidden_f, layer2_neigh.astype(jnp.float32), precision=maximal_precision)
    logits = scores.astype(jnp.bfloat16).reshape(N_WIDE, N_NARROW, ROWS_DEV, CLS)
    grad_f = grad_logits.reshape(devices, ROWS_DEV, CLS).astype(jnp.float32)
    grad_self2 = jnp.einsum("drh,drc->hc", hidden_f, grad_f, precision=maximal_precision)
    grad_neigh2 = jnp.einsum("drh,drc->hc", agg_hidden_f, grad_f, precision=maximal_precision)
    grad_agg = jnp.einsum("drc,hc->drh", grad_f, layer2_neigh.astype(jnp.float32), precision=maximal_precision)
    grad_ext = lax.map(one_back, (flat_tiles, flat_index, grad_agg))
    remote = grad_ext[:, ROWS_DEV:].reshape(N_WIDE, N_NARROW, N_WIDE, SLOT, HID).transpose(2, 1, 0, 3, 4)
    remote = remote.reshape(devices, N_WIDE * SLOT, HID)
    remote = jnp.where(live_slot[..., None], remote, jnp.zeros((), remote.dtype))
    from_peers = jax.vmap(add_rows)(flat_rows, remote)
    grad_hidden = jnp.einsum("drc,hc->drh", grad_f, layer2_self.astype(jnp.float32), precision=maximal_precision)
    grad_hidden = grad_hidden + grad_ext[:, :ROWS_DEV] + from_peers
    grad_pre = jnp.where(preactivation_values > 0, grad_hidden, jnp.zeros((), grad_hidden.dtype)).astype(jnp.bfloat16)
    preactivation_gradient_flat = grad_pre.astype(jnp.float32)
    first_self_weight_gradient = jnp.einsum("pou,poy->uy", flattened_vertex_features.astype(jnp.float32), preactivation_gradient_flat, precision=maximal_precision)
    first_neighbour_weight_gradient = jnp.einsum("pou,poy->uy", neighbour_feature_sum.astype(jnp.float32), preactivation_gradient_flat, precision=maximal_precision)
    grad_bias1 = jnp.sum(preactivation_gradient_flat, axis=(0, 1))
    return (logits, first_self_weight_gradient, first_neighbour_weight_gradient, grad_bias1, grad_self2, grad_neigh2)
```

```python
import jax
import jax.numpy as jnp
from jax import lax
from jax.experimental import pallas as pl
from jax.experimental.pallas import tpu as pltpu
from jax.sharding import Mesh, PartitionSpec as P

BF = jnp.bfloat16
F32 = jnp.float32
PLANE = ("x", "core", "y")
WIDE = ("z", "x", "core")
VM = pl.BlockSpec(memory_space=pltpu.VMEM)
SM = pl.BlockSpec(memory_space=pltpu.SMEM)
PARAMS = pltpu.CompilerParams(vmem_limit_bytes=32 * 1024 * 1024)


def dot(a, b):
    return jnp.dot(a, b, preferred_element_type=F32)


def dot_nt(a, b):
    return lax.dot_general(a, b, (((1,), (1,)), ((), ())), preferred_element_type=F32)


def split(values):
    upper = values.astype(BF)
    return upper, (values - upper.astype(F32)).astype(BF)


def before_kernel(index, rows, counts, feat, tiles, grad_t, send, pick, own_t, acc, padded):
    slot = lax.broadcasted_iota(jnp.int32, (2, 128), 0)
    wanted = jnp.where(slot < counts[...], rows[...], 512)
    by_slot = jnp.concatenate([wanted[0:1, :], wanted[1:2, :]], axis=1)
    i = lax.broadcasted_iota(jnp.int32, (256, 256), 0)
    j = lax.broadcasted_iota(jnp.int32, (256, 256), 1)
    place = jnp.where(j < 128, j * 2, (j - 128) * 2 + 1)
    perm = jnp.where(i == place, 1.0, 0.0).astype(BF)
    wide_rows = jnp.broadcast_to(by_slot, (128, 256))
    half = wide_rows // 2
    low = wide_rows - half * 2
    column = 2.0 * dot_nt(perm, half.astype(F32).astype(BF)) + dot_nt(perm, low.astype(F32).astype(BF))
    lane = lax.broadcasted_iota(jnp.int32, (256, 128), 1).astype(F32)
    for c in range(4):
        pick[:, c * 128 : (c + 1) * 128] = jnp.where(column == lane + 128.0 * c, 1.0, 0.0).astype(BF)
    send[:, 0:128] = dot(pick[...], feat[...]).astype(BF)
    padded[...] = jnp.zeros_like(padded)
    padded[0:172, :] = grad_t[...]
    acc[...] = jnp.zeros_like(acc)
    for b in range(4):
        part = padded[:, b * 128 : (b + 1) * 128]
        for k in range(3):
            e = index[b * 3 + k]
            acc[e] += dot(part, tiles[b * 3 + k])
    for b in range(4):
        own_t[:, b * 128 : (b + 1) * 128] = acc[b]
    for b in range(2):
        send[b * 128 : (b + 1) * 128, 128:384] = acc[4 + b].T.astype(BF)


def middle_kernel(
    index, recv, feat, tiles, pick, own_t, grad_t, w1s, w1n, bias, w2s_t, w2n_t,
    hidden, send, grads, ext, both, padded, wide_w,
):
    for b in range(4):
        ext[b] = feat[b * 128 : (b + 1) * 128, :]
    for b in range(2):
        ext[4 + b] = recv[b * 128 : (b + 1) * 128, 0:128]
    both[:, 0:128] = feat[...]
    for b in range(4):
        total = dot(tiles[b * 3], ext[index[b * 3]])
        total += dot(tiles[b * 3 + 1], ext[index[b * 3 + 1]])
        total += dot(tiles[b * 3 + 2], ext[index[b * 3 + 2]])
        both[b * 128 : (b + 1) * 128, 128:256] = total.astype(BF)
    pre = dot(both[:, 0:128], w1s[...]) + dot(both[:, 128:256], w1n[...]) + bias[...]
    hid = jnp.maximum(pre, 0.0).astype(BF)
    hidden[...] = hid
    send[...] = dot(pick[...], hid).astype(BF)
    padded[...] = jnp.zeros_like(padded)
    padded[0:172, :] = grad_t[...]
    wide_w[...] = jnp.zeros_like(wide_w)
    wide_w[0:172, :] = w2s_t[...]
    wide_w[256 : 256 + 172, :] = w2n_t[...]
    returned_t = recv[:, 128:384].astype(F32).T.astype(BF)
    back_t = own_t[...] + dot(returned_t, pick[...])
    upper_t, lower_t = split(back_t)
    upper, lower = split(back_t.T)
    grad = padded[...]
    grad_hidden = dot(grad.astype(F32).T.astype(BF), wide_w[0:256, :])
    grad_hidden += dot(upper, wide_w[256:512, :]) + dot(lower, wide_w[256:512, :])
    grad_pre = jnp.where(pre > 0, grad_hidden, 0.0).astype(BF)
    first = dot(both[...].astype(F32).T.astype(BF), grad_pre)
    bias_sum = jnp.sum(grad_pre.astype(F32), axis=0, keepdims=True)
    self2 = dot(grad, hid)
    neigh2 = dot(upper_t, hid) + dot(lower_t, hid)
    row = lax.broadcasted_iota(jnp.int32, (176, 256), 0)
    self2 = jnp.where(row == 172, bias_sum, self2[0:176, :])
    neigh2 = neigh2[0:176, :]
    for h in range(2):
        cols = slice(h * 128, (h + 1) * 128)
        base = h * 640
        grads[base : base + 256, :] = first[:, cols].astype(BF)
        grads[base + 256 : base + 432, :] = self2[:, cols].astype(BF)
        grads[base + 432 : base + 608, :] = neigh2[:, cols].astype(BF)
        grads[base + 608 : base + 640, :] = jnp.zeros((32, 128), BF)


def logits_kernel(index, recv, hidden, tiles, w2s_t, w2n_t, out_t, ext, agg):
    for b in range(4):
        ext[b] = hidden[b * 128 : (b + 1) * 128, :]
    for b in range(2):
        ext[4 + b] = recv[b * 128 : (b + 1) * 128, :]
    for b in range(4):
        total = dot(tiles[b * 3], ext[index[b * 3]])
        total += dot(tiles[b * 3 + 1], ext[index[b * 3 + 1]])
        total += dot(tiles[b * 3 + 2], ext[index[b * 3 + 2]])
        agg[b * 128 : (b + 1) * 128, :] = total.astype(BF)
    scores = dot_nt(w2s_t[...], hidden[...]) + dot_nt(w2n_t[...], agg[...])
    out_t[...] = scores.astype(BF)


def finish_kernel(total, self1, neigh1, bias, self2_t, neigh2_t):
    for h in range(2):
        cols = slice(h * 128, (h + 1) * 128)
        base = h * 640
        self1[:, cols] = total[base : base + 128, :].astype(F32)
        neigh1[:, cols] = total[base + 128 : base + 256, :].astype(F32)
        self2 = total[base + 256 : base + 432, :].astype(F32)
        self2_t[:, cols] = self2[0:172, :]
        bias[:, cols] = self2[172:173, :]
        neigh2_t[:, cols] = total[base + 432 : base + 608, :].astype(F32)[0:172, :]


def shape(dims, dtype):
    return jax.ShapeDtypeStruct(dims, dtype)


def before(index, rows, counts, feat, tiles, grad_t):
    return pl.pallas_call(
        before_kernel,
        out_shape=(shape((256, 384), BF), shape((256, 512), BF), shape((256, 512), F32)),
        in_specs=[SM, VM, VM, VM, VM, VM],
        out_specs=(VM, VM, VM),
        scratch_shapes=[pltpu.VMEM((6, 256, 128), F32), pltpu.VMEM((256, 512), BF)],
        compiler_params=PARAMS,
    )(index, rows, counts, feat, tiles, grad_t)


def middle(index, recv, feat, tiles, pick, own_t, grad_t, w1s, w1n, bias, w2s_t, w2n_t):
    return pl.pallas_call(
        middle_kernel,
        out_shape=(shape((512, 256), BF), shape((256, 256), BF), shape((1280, 128), BF)),
        in_specs=[SM] + [VM] * 11,
        out_specs=(VM, VM, VM),
        scratch_shapes=[
            pltpu.VMEM((6, 128, 128), BF),
            pltpu.VMEM((512, 256), BF),
            pltpu.VMEM((256, 512), BF),
            pltpu.VMEM((512, 256), BF),
        ],
        compiler_params=PARAMS,
    )(index, recv, feat, tiles, pick, own_t, grad_t, w1s, w1n, bias, w2s_t, w2n_t)


def scores(index, recv, hidden, tiles, w2s_t, w2n_t):
    return pl.pallas_call(
        logits_kernel,
        out_shape=shape((172, 512), BF),
        in_specs=[SM] + [VM] * 5,
        out_specs=VM,
        scratch_shapes=[pltpu.VMEM((6, 128, 256), BF), pltpu.VMEM((512, 256), BF)],
        compiler_params=PARAMS,
    )(index, recv, hidden, tiles, w2s_t, w2n_t)


def finish(total):
    return pl.pallas_call(
        finish_kernel,
        out_shape=(
            shape((128, 256), F32),
            shape((128, 256), F32),
            shape((1, 256), F32),
            shape((172, 256), F32),
            shape((172, 256), F32),
        ),
        in_specs=[VM],
        out_specs=(VM,) * 5,
        compiler_params=PARAMS,
    )(total)


def exchange(values, axes):
    return lax.all_to_all(values, axes, split_axis=0, concat_axis=0, tiled=True)


def shards(
    features,
    send_rows,
    send_counts,
    tile_index,
    tile_weight,
    first_layer_self_weight,
    first_layer_neighbour_weight,
    layer1_bias,
    layer2_self,
    layer2_neigh,
    grad_logits,
):
    feat = features.reshape(512, 128)
    rows = jnp.swapaxes(send_rows.reshape(128, 2), 0, 1)
    counts = send_counts.reshape(1, 128)
    index = tile_index.reshape(12)
    tiles = tile_weight.reshape(12, 128, 128)
    grad_t = jnp.swapaxes(grad_logits.reshape(512, 172), 0, 1)
    w2s_t = jnp.swapaxes(layer2_self, 0, 1)
    w2n_t = jnp.swapaxes(layer2_neigh, 0, 1)
    bias = layer1_bias.reshape(1, 256)

    send1, pick, own_t = before(index, rows, counts, feat, tiles, grad_t)
    recv1 = exchange(send1.reshape(128, 2, 384), WIDE).reshape(256, 384)
    hidden, send2, grads = middle(
        index, recv1, feat, tiles, pick, own_t, grad_t,
        first_layer_self_weight, first_layer_neighbour_weight, bias, w2s_t, w2n_t,
    )

    parts = exchange(grads.reshape(32, 40, 128), PLANE)
    recv2 = exchange(send2.reshape(128, 2, 256), WIDE).reshape(256, 256)
    chunk = jnp.sum(parts.astype(F32), axis=0).astype(BF)
    layers = exchange(jnp.broadcast_to(chunk[None], (16, 40, 128)), "z")
    chunk = jnp.sum(layers.astype(F32), axis=0).astype(BF)
    total = exchange(jnp.broadcast_to(chunk[None], (32, 40, 128)), PLANE)
    logits_t = scores(index, recv2, hidden, tiles, w2s_t, w2n_t)
    self1, neigh1, bias1, self2_t, neigh2_t = finish(total.reshape(1280, 128))
    logits = jnp.swapaxes(logits_t, 0, 1).reshape(1, 1, 512, 172)
    return (
        logits,
        self1,
        neigh1,
        bias1.reshape(256),
        jnp.swapaxes(self2_t, 0, 1),
        jnp.swapaxes(neigh2_t, 0, 1),
    )


def solution(mesh):
    fine = Mesh(mesh.devices.reshape(16, 4, 2, 4), ("z", "x", "core", "y"))
    return jax.shard_map(
        shards,
        mesh=fine,
        in_specs=(
            P(WIDE, "y", None, None),
            P(WIDE, "y", None, None),
            P(WIDE, "y", None),
            P(WIDE, "y", None, None),
            P(WIDE, "y", None, None, None, None),
            P(),
            P(),
            P(),
            P(),
            P(),
            P(WIDE, "y", None, None),
        ),
        out_specs=(P(WIDE, "y", None, None), P(), P(), P(), P(), P()),
        check_vma=False,
    )
```

```python
import jax
import jax.numpy as jnp
from jax import lax
from jax.experimental import pallas as pl
from jax.experimental.pallas import tpu as pltpu
from jax.sharding import Mesh, PartitionSpec as P

BF = jnp.bfloat16
F32 = jnp.float32
PLANE = ("x", "core", "y")
WIDE = ("z", "x", "core")
VM = pl.BlockSpec(memory_space=pltpu.VMEM)
SM = pl.BlockSpec(memory_space=pltpu.SMEM)
PARAMS = pltpu.CompilerParams(vmem_limit_bytes=32 * 1024 * 1024)


def dot(a, b):
    return jnp.dot(a, b, preferred_element_type=F32)


def dot_nt(a, b):
    return lax.dot_general(a, b, (((1,), (1,)), ((), ())), preferred_element_type=F32)


def split(values):
    upper = values.astype(BF)
    return upper, (values - upper.astype(F32)).astype(BF)


def before_kernel(*refs):
    rows_in, counts_in = refs[0:2]
    send, pick, own_t = refs[11:14]
    feat, grad_t, tiles = refs[14:17]
    rows, counts, index, acc, padded, sems = refs[23:29]
    pairs = [(rows_in, rows), (counts_in, counts)] + list(zip(refs[2:11], refs[14:23])) + [(refs[10], index)]
    copies = [pltpu.make_async_copy(a, b, sems.at[i]) for i, (a, b) in enumerate(pairs)]
    for copy in copies:
        copy.start()
    acc[...] = jnp.zeros_like(acc)
    padded[...] = jnp.zeros_like(padded)
    i = lax.broadcasted_iota(jnp.int32, (256, 256), 0)
    j = lax.broadcasted_iota(jnp.int32, (256, 256), 1)
    place = jnp.where(j < 128, j * 2, (j - 128) * 2 + 1)
    perm = jnp.where(i == place, 1.0, 0.0).astype(BF)
    copies[0].wait()
    copies[1].wait()
    slot = lax.broadcasted_iota(jnp.int32, (2, 128), 0)
    wanted = jnp.where(slot < counts[...], rows[...], 512)
    by_slot = jnp.concatenate([wanted[0:1, :], wanted[1:2, :]], axis=1)
    wide_rows = jnp.broadcast_to(by_slot, (128, 256))
    half = wide_rows // 2
    low = wide_rows - half * 2
    column = 2.0 * dot_nt(perm, half.astype(F32).astype(BF)) + dot_nt(perm, low.astype(F32).astype(BF))
    lane = lax.broadcasted_iota(jnp.int32, (256, 128), 1).astype(F32)
    for c in range(4):
        pick[:, c * 128 : (c + 1) * 128] = jnp.where(column == lane + 128.0 * c, 1.0, 0.0).astype(BF)
    copies[2].wait()
    send[:, 0:128] = dot(pick[...], feat[...]).astype(BF)
    copies[3].wait()
    padded[0:172, :] = grad_t[...]
    copies[4].wait()
    copies[11].wait()
    for b in range(4):
        part = padded[:, b * 128 : (b + 1) * 128]
        for k in range(3):
            e = index[k, 0, b]
            acc[e] += dot(part, tiles[b * 3 + k])
    for b in range(4):
        own_t[:, b * 128 : (b + 1) * 128] = acc[b]
    for b in range(2):
        send[b * 128 : (b + 1) * 128, 128:384] = acc[4 + b].T.astype(BF)
    for copy in copies[5:11]:
        copy.wait()


def gather_tiles(index, tiles, ext, b):
    total = dot(tiles[b * 3], ext[index[0, 0, b]])
    total += dot(tiles[b * 3 + 1], ext[index[1, 0, b]])
    total += dot(tiles[b * 3 + 2], ext[index[2, 0, b]])
    return total.astype(BF)


def middle_kernel(
    index, recv, feat, tiles, pick, own_t, grad_t, w1s, w1n, bias, w2s_t, w2n_t,
    hidden, out, ext, both, padded, wide_w, grads,
):
    for b in range(4):
        ext[b] = feat[b * 128 : (b + 1) * 128, :]
    for b in range(2):
        ext[4 + b] = recv[b * 128 : (b + 1) * 128, 0:128]
    both[:, 0:128] = feat[...]
    for b in range(4):
        both[b * 128 : (b + 1) * 128, 128:256] = gather_tiles(index, tiles, ext, b)
    pre = dot(both[:, 0:128], w1s[...]) + dot(both[:, 128:256], w1n[...]) + bias[...]
    hid = jnp.maximum(pre, 0.0).astype(BF)
    hidden[...] = hid
    i = lax.broadcasted_iota(jnp.int32, (256, 256), 0)
    j = lax.broadcasted_iota(jnp.int32, (256, 256), 1)
    place = ((i // 2) % 16) * 16 + (i // 32) * 2 + i % 2
    perm = jnp.where(j == place, 1.0, 0.0).astype(BF)
    picked = dot(perm, dot(pick[...], hid).astype(BF)).astype(BF)
    for p in range(8):
        out[p, 160:192, :] = picked[p * 32 : (p + 1) * 32, 0:128]
        out[p, 192:224, :] = picked[p * 32 : (p + 1) * 32, 128:256]
    padded[...] = jnp.zeros_like(padded)
    padded[0:172, :] = grad_t[...]
    wide_w[...] = jnp.zeros_like(wide_w)
    wide_w[0:172, :] = w2s_t[...]
    wide_w[256 : 256 + 172, :] = w2n_t[...]
    returned_t = recv[:, 128:384].astype(F32).T.astype(BF)
    back_t = own_t[...] + dot(returned_t, pick[...])
    upper_t, lower_t = split(back_t)
    upper, lower = split(back_t.T)
    grad = padded[...]
    grad_hidden = dot(grad.astype(F32).T.astype(BF), wide_w[0:256, :])
    grad_hidden += dot(upper, wide_w[256:512, :]) + dot(lower, wide_w[256:512, :])
    grad_pre = jnp.where(pre > 0, grad_hidden, 0.0).astype(BF)
    first = dot(both[...].astype(F32).T.astype(BF), grad_pre)
    bias_sum = jnp.sum(grad_pre.astype(F32), axis=0, keepdims=True)
    self2 = dot(grad, hid)
    neigh2 = dot(upper_t, hid) + dot(lower_t, hid)
    row = lax.broadcasted_iota(jnp.int32, (176, 256), 0)
    self2 = jnp.where(row == 172, bias_sum, self2[0:176, :])
    neigh2 = neigh2[0:176, :]
    for h in range(2):
        cols = slice(h * 128, (h + 1) * 128)
        base = h * 640
        grads[base : base + 256, :] = first[:, cols].astype(BF)
        grads[base + 256 : base + 432, :] = self2[:, cols].astype(BF)
        grads[base + 432 : base + 608, :] = neigh2[:, cols].astype(BF)
        grads[base + 608 : base + 640, :] = jnp.zeros((32, 128), BF)
    for p in range(8):
        out[p, 0:160, :] = grads[p * 160 : (p + 1) * 160, :]


def plane_kernel(parts, chunk, hidden):
    total = parts[0, 0:160, :].astype(F32)
    for p in range(1, 8):
        total += parts[p, 0:160, :].astype(F32)
    total = total.astype(BF)
    for q in range(4):
        chunk[q] = total[q * 40 : (q + 1) * 40, :]
    i = lax.broadcasted_iota(jnp.int32, (256, 256), 0)
    j = lax.broadcasted_iota(jnp.int32, (256, 256), 1)
    place = ((i // 2) % 8) * 32 + (i // 16) * 2 + i % 2
    perm = jnp.where(j == place, 1.0, 0.0).astype(BF)
    for h in range(2):
        rows = jnp.concatenate([parts[p, 160 + h * 32 : 192 + h * 32, :] for p in range(8)], axis=0)
        hidden[:, h * 128 : (h + 1) * 128] = dot(perm, rows).astype(BF)


def column_kernel(parts, hidden, out):
    total = parts[0].astype(F32)
    for p in range(1, 4):
        total += parts[p].astype(F32)
    total = total.astype(BF)
    for z in range(16):
        out[z, 0:16, :] = hidden[z * 16 : (z + 1) * 16, 0:128]
        out[z, 16:32, :] = hidden[z * 16 : (z + 1) * 16, 128:256]
        out[z, 32:72, :] = total


def layer_kernel(parts, out):
    total = parts[0, 32:72, :].astype(F32)
    for p in range(1, 16):
        total += parts[p, 32:72, :].astype(F32)
    total = total.astype(BF)
    for p in range(32):
        out[p] = total


def logits_kernel(index, recv, hidden, tiles, w2s_t, w2n_t, out_t, ext, agg):
    for b in range(4):
        ext[b] = hidden[b * 128 : (b + 1) * 128, :]
    for z in range(16):
        rows = slice((z % 8) * 16, (z % 8) * 16 + 16)
        ext[4 + z // 8, rows, 0:128] = recv[z, 0:16, :]
        ext[4 + z // 8, rows, 128:256] = recv[z, 16:32, :]
    for b in range(4):
        agg[b * 128 : (b + 1) * 128, :] = gather_tiles(index, tiles, ext, b)
    scores = dot_nt(w2s_t[...], hidden[...]) + dot_nt(w2n_t[...], agg[...])
    out_t[...] = scores.astype(BF)


def finish_kernel(total, self1, neigh1, bias, self2_t, neigh2_t):
    for h in range(2):
        cols = slice(h * 128, (h + 1) * 128)
        base = h * 640
        self1[:, cols] = total[base : base + 128, :].astype(F32)
        neigh1[:, cols] = total[base + 128 : base + 256, :].astype(F32)
        self2 = total[base + 256 : base + 432, :].astype(F32)
        self2_t[:, cols] = self2[0:172, :]
        bias[:, cols] = self2[172:173, :]
        neigh2_t[:, cols] = total[base + 432 : base + 608, :].astype(F32)[0:172, :]


def shape(dims, dtype):
    return jax.ShapeDtypeStruct(dims, dtype)


def before(rows, counts, *kept):
    here = [pltpu.with_memory_space_constraint(value, pltpu.HBM) for value in (rows, counts) + kept]
    return pl.pallas_call(
        before_kernel,
        out_shape=(shape((256, 384), BF), shape((256, 512), BF), shape((256, 512), F32))
        + tuple(shape(value.shape, value.dtype) for value in kept),
        in_specs=[pl.BlockSpec(memory_space=pltpu.HBM)] * 11,
        out_specs=(VM,) * 12,
        scratch_shapes=[
            pltpu.VMEM((2, 128), jnp.int32),
            pltpu.VMEM((1, 128), jnp.int32),
            pltpu.SMEM((3, 1, 4), jnp.int32),
            pltpu.VMEM((6, 256, 128), F32),
            pltpu.VMEM((256, 512), BF),
            pltpu.SemaphoreType.DMA((12,)),
        ],
        compiler_params=PARAMS,
    )(*here)


def middle(index, recv, feat, tiles, pick, own_t, grad_t, w1s, w1n, bias, w2s_t, w2n_t):
    return pl.pallas_call(
        middle_kernel,
        out_shape=(shape((512, 256), BF), shape((8, 224, 128), BF)),
        in_specs=[SM] + [VM] * 11,
        out_specs=(VM, VM),
        scratch_shapes=[
            pltpu.VMEM((6, 128, 128), BF),
            pltpu.VMEM((512, 256), BF),
            pltpu.VMEM((256, 512), BF),
            pltpu.VMEM((512, 256), BF),
            pltpu.VMEM((1280, 128), BF),
        ],
        compiler_params=PARAMS,
    )(index, recv, feat, tiles, pick, own_t, grad_t, w1s, w1n, bias, w2s_t, w2n_t)


def scores(index, recv, hidden, tiles, w2s_t, w2n_t):
    return pl.pallas_call(
        logits_kernel,
        out_shape=shape((172, 512), BF),
        in_specs=[SM] + [VM] * 5,
        out_specs=VM,
        scratch_shapes=[pltpu.VMEM((6, 128, 256), BF), pltpu.VMEM((512, 256), BF)],
        compiler_params=PARAMS,
    )(index, recv, hidden, tiles, w2s_t, w2n_t)


def after_plane(parts):
    return pl.pallas_call(
        plane_kernel,
        out_shape=(shape((4, 40, 128), BF), shape((256, 256), BF)),
        in_specs=[VM],
        out_specs=(VM, VM),
        compiler_params=PARAMS,
    )(parts)


def after_column(parts, hidden):
    return pl.pallas_call(
        column_kernel,
        out_shape=shape((16, 72, 128), BF),
        in_specs=[VM, VM],
        out_specs=VM,
        compiler_params=PARAMS,
    )(parts, hidden)


def after_layers(parts):
    return pl.pallas_call(
        layer_kernel,
        out_shape=shape((32, 40, 128), BF),
        in_specs=[VM],
        out_specs=VM,
        compiler_params=PARAMS,
    )(parts)


def finish(total):
    return pl.pallas_call(
        finish_kernel,
        out_shape=(
            shape((128, 256), F32),
            shape((128, 256), F32),
            shape((1, 256), F32),
            shape((172, 256), F32),
            shape((172, 256), F32),
        ),
        in_specs=[VM],
        out_specs=(VM,) * 5,
        compiler_params=PARAMS,
    )(total)


def exchange(values, axes):
    return lax.all_to_all(values, axes, split_axis=0, concat_axis=0, tiled=True)


def shards(
    features,
    send_rows,
    send_counts,
    tile_index,
    tile_weight,
    first_layer_self_weight,
    first_layer_neighbour_weight,
    layer1_bias,
    layer2_self,
    layer2_neigh,
    grad_logits,
):
    feat = features.reshape(512, 128)
    rows = jnp.swapaxes(send_rows.reshape(128, 2), 0, 1)
    counts = send_counts.reshape(1, 128)
    index = jnp.transpose(tile_index, (0, 3, 1, 2)).reshape(3, 1, 4)
    tiles = tile_weight.reshape(12, 128, 128)
    grad_t = jnp.swapaxes(grad_logits.reshape(512, 172), 0, 1)
    w2s_t = jnp.swapaxes(layer2_self, 0, 1)
    w2n_t = jnp.swapaxes(layer2_neigh, 0, 1)
    bias = layer1_bias.reshape(1, 256)

    send1, pick, own_t, feat, grad_t, tiles, w1s, w1n, bias, w2s_t, w2n_t, index = before(
        rows, counts, feat, grad_t, tiles,
        first_layer_self_weight, first_layer_neighbour_weight, bias, w2s_t, w2n_t, index,
    )
    recv1 = exchange(send1.reshape(128, 2, 384), WIDE).reshape(256, 384)
    hidden, parts = middle(
        index, recv1, feat, tiles, pick, own_t, grad_t,
        w1s, w1n, bias, w2s_t, w2n_t,
    )
    chunk, passing = after_plane(exchange(parts, ("x", "core")))
    recv2 = exchange(after_column(exchange(chunk, "y"), passing), "z")
    total = exchange(after_layers(recv2), PLANE)
    logits_t = scores(index, recv2, hidden, tiles, w2s_t, w2n_t)
    self1, neigh1, bias1, self2_t, neigh2_t = finish(total.reshape(1280, 128))
    logits = jnp.swapaxes(logits_t, 0, 1).reshape(1, 1, 512, 172)
    return (
        logits,
        self1,
        neigh1,
        bias1.reshape(256),
        jnp.swapaxes(self2_t, 0, 1),
        jnp.swapaxes(neigh2_t, 0, 1),
    )


def solution(mesh):
    fine = Mesh(mesh.devices.reshape(16, 4, 2, 4), ("z", "x", "core", "y"))
    return jax.shard_map(
        shards,
        mesh=fine,
        in_specs=(
            P(WIDE, "y", None, None),
            P(WIDE, "y", None, None),
            P(WIDE, "y", None),
            P(WIDE, "y", None, None),
            P(WIDE, "y", None, None, None, None),
            P(),
            P(),
            P(),
            P(),
            P(),
            P(WIDE, "y", None, None),
        ),
        out_specs=(P(WIDE, "y", None, None), P(), P(), P(), P(), P()),
        check_vma=False,
    )
```

```python
import jax
import jax.numpy as jnp
from jax import lax
from jax.experimental import pallas as pl
from jax.experimental.pallas import tpu as pltpu
from jax.sharding import Mesh, PartitionSpec as P

BF = jnp.bfloat16
F32 = jnp.float32
EVERY = ("z", "x", "core", "y")
WIDE = ("z", "x", "core")
DIAGONALS = [[z * 4 + (g + z) % 4 for z in range(16)] for g in range(4)]
PLANES = [[z * 32 + xc * 4 + (g + z) % 4 for xc in range(8) for g in range(4)] for z in range(16)]
VM = pl.BlockSpec(memory_space=pltpu.VMEM)
SM = pl.BlockSpec(memory_space=pltpu.SMEM)
PARAMS = pltpu.CompilerParams(vmem_limit_bytes=32 * 1024 * 1024)


def dot(a, b):
    return jnp.dot(a, b, preferred_element_type=F32)


def dot_nt(a, b):
    return lax.dot_general(a, b, (((1,), (1,)), ((), ())), preferred_element_type=F32)


def split(values):
    upper = values.astype(BF)
    return upper, (values - upper.astype(F32)).astype(BF)


def place():
    return lax.axis_index("z"), lax.axis_index("y")


def before_kernel(*refs):
    rows_in, counts_in = refs[0:2]
    send, pick, own_t = refs[11:14]
    feat, grad_t, tiles = refs[14:17]
    rows, counts, index, acc, padded, sems = refs[23:29]
    pairs = [(rows_in, rows), (counts_in, counts)] + list(zip(refs[2:11], refs[14:23])) + [(refs[10], index)]
    copies = [pltpu.make_async_copy(a, b, sems.at[i]) for i, (a, b) in enumerate(pairs)]
    for copy in copies:
        copy.start()
    acc[...] = jnp.zeros_like(acc)
    padded[...] = jnp.zeros_like(padded)
    i = lax.broadcasted_iota(jnp.int32, (256, 256), 0)
    j = lax.broadcasted_iota(jnp.int32, (256, 256), 1)
    place = jnp.where(j < 128, j * 2, (j - 128) * 2 + 1)
    perm = jnp.where(i == place, 1.0, 0.0).astype(BF)
    copies[0].wait()
    copies[1].wait()
    slot = lax.broadcasted_iota(jnp.int32, (2, 128), 0)
    wanted = jnp.where(slot < counts[...], rows[...], 512)
    by_slot = jnp.concatenate([wanted[0:1, :], wanted[1:2, :]], axis=1)
    wide_rows = jnp.broadcast_to(by_slot, (128, 256))
    half = wide_rows // 2
    low = wide_rows - half * 2
    column = 2.0 * dot_nt(perm, half.astype(F32).astype(BF)) + dot_nt(perm, low.astype(F32).astype(BF))
    lane = lax.broadcasted_iota(jnp.int32, (256, 128), 1).astype(F32)
    for c in range(4):
        pick[:, c * 128 : (c + 1) * 128] = jnp.where(column == lane + 128.0 * c, 1.0, 0.0).astype(BF)
    copies[2].wait()
    send[:, 0:128] = dot(pick[...], feat[...]).astype(BF)
    copies[3].wait()
    padded[0:172, :] = grad_t[...]
    copies[4].wait()
    copies[11].wait()
    for b in range(4):
        part = padded[:, b * 128 : (b + 1) * 128]
        for k in range(3):
            e = index[k, 0, b]
            acc[e] += dot(part, tiles[b * 3 + k])
    for b in range(4):
        own_t[:, b * 128 : (b + 1) * 128] = acc[b]
    for b in range(2):
        send[b * 128 : (b + 1) * 128, 128:384] = acc[4 + b].T.astype(BF)
    for copy in copies[5:11]:
        copy.wait()


def gather_tiles(index, tiles, ext, b):
    total = dot(tiles[b * 3], ext[index[0, 0, b]])
    total += dot(tiles[b * 3 + 1], ext[index[1, 0, b]])
    total += dot(tiles[b * 3 + 2], ext[index[2, 0, b]])
    return total.astype(BF)


def middle_kernel(
    index, recv, feat, tiles, pick, own_t, grad_t, w1s, w1n, bias, w2s_t, w2n_t,
    hidden, out, ext, both, padded, wide_w, grads, perm,
):
    for b in range(4):
        ext[b] = feat[b * 128 : (b + 1) * 128, :]
    for b in range(2):
        ext[4 + b] = recv[b * 128 : (b + 1) * 128, 0:128]
    both[:, 0:128] = feat[...]
    for b in range(4):
        both[b * 128 : (b + 1) * 128, 128:256] = gather_tiles(index, tiles, ext, b)
    pre = dot(both[:, 0:128], w1s[...]) + dot(both[:, 128:256], w1n[...]) + bias[...]
    hid = jnp.maximum(pre, 0.0).astype(BF)
    hidden[...] = hid
    y = place()[1]
    i = lax.broadcasted_iota(jnp.int32, (512, 128), 0)
    z2 = ((y - (i >> 4)) & 3) + 4 * ((i >> 1) & 3)
    source = ((i >> 3) & 1) * 256 + z2 * 16 + (i >> 6) * 2 + (i & 1)
    lane = lax.broadcasted_iota(jnp.int32, (512, 128), 1)
    for c in range(4):
        perm[:, c * 128 : (c + 1) * 128] = jnp.where(source == lane + 128 * c, 1.0, 0.0).astype(BF)
    picked = dot(pick[...], hid).astype(BF)
    picked = jnp.concatenate([picked[:, 0:128], picked[:, 128:256]], axis=0)
    picked = dot(perm[...], picked).astype(BF)
    for p in range(32):
        out[p, 0:16, :] = picked[p * 16 : (p + 1) * 16, :]
    padded[...] = jnp.zeros_like(padded)
    padded[0:172, :] = grad_t[...]
    wide_w[...] = jnp.zeros_like(wide_w)
    wide_w[0:172, :] = w2s_t[...]
    wide_w[256 : 256 + 172, :] = w2n_t[...]
    returned_t = recv[:, 128:384].astype(F32).T.astype(BF)
    back_t = own_t[...] + dot(returned_t, pick[...])
    upper_t, lower_t = split(back_t)
    upper, lower = split(back_t.T)
    grad = padded[...]
    grad_hidden = dot(grad.astype(F32).T.astype(BF), wide_w[0:256, :])
    grad_hidden += dot(upper, wide_w[256:512, :]) + dot(lower, wide_w[256:512, :])
    grad_pre = jnp.where(pre > 0, grad_hidden, 0.0).astype(BF)
    first = dot(both[...].astype(F32).T.astype(BF), grad_pre)
    bias_sum = jnp.sum(grad_pre.astype(F32), axis=0, keepdims=True)
    self2 = dot(grad, hid)
    neigh2 = dot(upper_t, hid) + dot(lower_t, hid)
    row = lax.broadcasted_iota(jnp.int32, (176, 256), 0)
    self2 = jnp.where(row == 172, bias_sum, self2[0:176, :])
    neigh2 = neigh2[0:176, :]
    for h in range(2):
        cols = slice(h * 128, (h + 1) * 128)
        base = h * 640
        grads[base : base + 256, :] = first[:, cols].astype(BF)
        grads[base + 256 : base + 432, :] = self2[:, cols].astype(BF)
        grads[base + 432 : base + 608, :] = neigh2[:, cols].astype(BF)
        grads[base + 608 : base + 640, :] = jnp.zeros((32, 128), BF)
    for p in range(32):
        out[p, 16:56, :] = grads[p * 40 : (p + 1) * 40, :]


def plane_kernel(parts, out, perm):
    total = parts[0, 16:56, :].astype(F32)
    for p in range(1, 32):
        total += parts[p, 16:56, :].astype(F32)
    total = total.astype(BF)
    z, y = place()
    i = lax.broadcasted_iota(jnp.int32, (512, 128), 0)
    z2 = i >> 5
    sender = ((i >> 1) & 7) * 4 + ((z2 + y - 2 * z) & 3)
    source = sender * 16 + ((i >> 4) & 1) * 8 + (z2 >> 2) * 2 + (i & 1)
    lane = lax.broadcasted_iota(jnp.int32, (512, 128), 1)
    for c in range(4):
        perm[:, c * 128 : (c + 1) * 128] = jnp.where(source == lane + 128 * c, 1.0, 0.0).astype(BF)
    rows = jnp.concatenate([parts[p, 0:16, :] for p in range(32)], axis=0)
    rows = dot(perm[...], rows).astype(BF)
    for z2 in range(16):
        out[z2, 0:32, :] = rows[z2 * 32 : (z2 + 1) * 32, :]
        out[z2, 32:72, :] = total


def layer_kernel(parts, out):
    total = parts[0, 32:72, :].astype(F32)
    for p in range(1, 16):
        total += parts[p, 32:72, :].astype(F32)
    total = total.astype(BF)
    for p in range(32):
        out[p] = total


def logits_kernel(index, recv, hidden, tiles, w2s_t, w2n_t, out_t, ext, agg):
    for b in range(4):
        ext[b] = hidden[b * 128 : (b + 1) * 128, :]
    for z in range(16):
        rows = slice((z % 8) * 16, (z % 8) * 16 + 16)
        ext[4 + z // 8, rows, 0:128] = recv[z, 0:16, :]
        ext[4 + z // 8, rows, 128:256] = recv[z, 16:32, :]
    for b in range(4):
        agg[b * 128 : (b + 1) * 128, :] = gather_tiles(index, tiles, ext, b)
    scores = dot_nt(w2s_t[...], hidden[...]) + dot_nt(w2n_t[...], agg[...])
    out_t[...] = scores.astype(BF)


def finish_kernel(total, self1, neigh1, bias, self2_t, neigh2_t):
    for h in range(2):
        cols = slice(h * 128, (h + 1) * 128)
        base = h * 640
        self1[:, cols] = total[base : base + 128, :].astype(F32)
        neigh1[:, cols] = total[base + 128 : base + 256, :].astype(F32)
        self2 = total[base + 256 : base + 432, :].astype(F32)
        self2_t[:, cols] = self2[0:172, :]
        bias[:, cols] = self2[172:173, :]
        neigh2_t[:, cols] = total[base + 432 : base + 608, :].astype(F32)[0:172, :]


def shape(dims, dtype):
    return jax.ShapeDtypeStruct(dims, dtype)


def before(rows, counts, *kept):
    here = [pltpu.with_memory_space_constraint(value, pltpu.HBM) for value in (rows, counts) + kept]
    return pl.pallas_call(
        before_kernel,
        out_shape=(shape((256, 384), BF), shape((256, 512), BF), shape((256, 512), F32))
        + tuple(shape(value.shape, value.dtype) for value in kept),
        in_specs=[pl.BlockSpec(memory_space=pltpu.HBM)] * 11,
        out_specs=(VM,) * 12,
        scratch_shapes=[
            pltpu.VMEM((2, 128), jnp.int32),
            pltpu.VMEM((1, 128), jnp.int32),
            pltpu.SMEM((3, 1, 4), jnp.int32),
            pltpu.VMEM((6, 256, 128), F32),
            pltpu.VMEM((256, 512), BF),
            pltpu.SemaphoreType.DMA((12,)),
        ],
        compiler_params=PARAMS,
    )(*here)


def middle(index, recv, feat, tiles, pick, own_t, grad_t, w1s, w1n, bias, w2s_t, w2n_t):
    return pl.pallas_call(
        middle_kernel,
        out_shape=(shape((512, 256), BF), shape((32, 56, 128), BF)),
        in_specs=[SM] + [VM] * 11,
        out_specs=(VM, VM),
        scratch_shapes=[
            pltpu.VMEM((6, 128, 128), BF),
            pltpu.VMEM((512, 256), BF),
            pltpu.VMEM((256, 512), BF),
            pltpu.VMEM((512, 256), BF),
            pltpu.VMEM((1280, 128), BF),
            pltpu.VMEM((512, 512), BF),
        ],
        compiler_params=PARAMS,
    )(index, recv, feat, tiles, pick, own_t, grad_t, w1s, w1n, bias, w2s_t, w2n_t)


def scores(index, recv, hidden, tiles, w2s_t, w2n_t):
    return pl.pallas_call(
        logits_kernel,
        out_shape=shape((172, 512), BF),
        in_specs=[SM] + [VM] * 5,
        out_specs=VM,
        scratch_shapes=[pltpu.VMEM((6, 128, 256), BF), pltpu.VMEM((512, 256), BF)],
        compiler_params=PARAMS,
    )(index, recv, hidden, tiles, w2s_t, w2n_t)


def after_plane(parts):
    return pl.pallas_call(
        plane_kernel,
        out_shape=shape((16, 72, 128), BF),
        in_specs=[VM],
        out_specs=VM,
        scratch_shapes=[pltpu.VMEM((512, 512), BF)],
        compiler_params=PARAMS,
    )(parts)


def after_layers(parts):
    return pl.pallas_call(
        layer_kernel,
        out_shape=shape((32, 40, 128), BF),
        in_specs=[VM],
        out_specs=VM,
        compiler_params=PARAMS,
    )(parts)


def finish(total):
    return pl.pallas_call(
        finish_kernel,
        out_shape=(
            shape((128, 256), F32),
            shape((128, 256), F32),
            shape((1, 256), F32),
            shape((172, 256), F32),
            shape((172, 256), F32),
        ),
        in_specs=[VM],
        out_specs=(VM,) * 5,
        compiler_params=PARAMS,
    )(total)


def exchange(values, axes, groups=None):
    return lax.all_to_all(values, axes, split_axis=0, concat_axis=0, axis_index_groups=groups, tiled=True)


def shards(
    features,
    send_rows,
    send_counts,
    tile_index,
    tile_weight,
    first_layer_self_weight,
    first_layer_neighbour_weight,
    layer1_bias,
    layer2_self,
    layer2_neigh,
    grad_logits,
):
    feat = features.reshape(512, 128)
    rows = jnp.swapaxes(send_rows.reshape(128, 2), 0, 1)
    counts = send_counts.reshape(1, 128)
    index = jnp.transpose(tile_index, (0, 3, 1, 2)).reshape(3, 1, 4)
    tiles = tile_weight.reshape(12, 128, 128)
    grad_t = jnp.swapaxes(grad_logits.reshape(512, 172), 0, 1)
    w2s_t = jnp.swapaxes(layer2_self, 0, 1)
    w2n_t = jnp.swapaxes(layer2_neigh, 0, 1)
    bias = layer1_bias.reshape(1, 256)

    send1, pick, own_t, feat, grad_t, tiles, w1s, w1n, bias, w2s_t, w2n_t, index = before(
        rows, counts, feat, grad_t, tiles,
        first_layer_self_weight, first_layer_neighbour_weight, bias, w2s_t, w2n_t, index,
    )
    recv1 = exchange(send1.reshape(128, 2, 384), WIDE).reshape(256, 384)
    hidden, parts = middle(
        index, recv1, feat, tiles, pick, own_t, grad_t,
        w1s, w1n, bias, w2s_t, w2n_t,
    )
    recv2 = exchange(after_plane(exchange(parts, EVERY, PLANES)), ("z", "y"), DIAGONALS)
    total = exchange(after_layers(recv2), EVERY, PLANES)
    logits_t = scores(index, recv2, hidden, tiles, w2s_t, w2n_t)
    self1, neigh1, bias1, self2_t, neigh2_t = finish(total.reshape(1280, 128))
    logits = jnp.swapaxes(logits_t, 0, 1).reshape(1, 1, 512, 172)
    return (
        logits,
        self1,
        neigh1,
        bias1.reshape(256),
        jnp.swapaxes(self2_t, 0, 1),
        jnp.swapaxes(neigh2_t, 0, 1),
    )


def solution(mesh):
    fine = Mesh(mesh.devices.reshape(16, 4, 2, 4), ("z", "x", "core", "y"))
    return jax.shard_map(
        shards,
        mesh=fine,
        in_specs=(
            P(WIDE, "y", None, None),
            P(WIDE, "y", None, None),
            P(WIDE, "y", None),
            P(WIDE, "y", None, None),
            P(WIDE, "y", None, None, None, None),
            P(),
            P(),
            P(),
            P(),
            P(),
            P(WIDE, "y", None, None),
        ),
        out_specs=(P(WIDE, "y", None, None), P(), P(), P(), P(), P()),
        check_vma=False,
    )
```

```python
import jax
import jax.numpy as jnp
from jax import lax
from jax.experimental import pallas as pl
from jax.experimental.pallas import tpu as pltpu
from jax.sharding import Mesh, PartitionSpec as P

BF = jnp.bfloat16
F32 = jnp.float32
PLANE = ("x", "core", "y")
WIDE = ("z", "x", "core")
VM = pl.BlockSpec(memory_space=pltpu.VMEM)
SM = pl.BlockSpec(memory_space=pltpu.SMEM)
PARAMS = pltpu.CompilerParams(vmem_limit_bytes=32 * 1024 * 1024)


def dot(a, b):
    return jnp.dot(a, b, preferred_element_type=F32)


def dot_nt(a, b):
    return lax.dot_general(a, b, (((1,), (1,)), ((), ())), preferred_element_type=F32)


def split(values):
    upper = values.astype(BF)
    return upper, (values - upper.astype(F32)).astype(BF)


def place():
    return lax.axis_index("y")


def before_kernel(*refs):
    rows_in, counts_in = refs[0:2]
    send, pick, own_t = refs[11:14]
    feat, grad_t, tiles = refs[14:17]
    rows, counts, index, acc, padded, sems = refs[23:29]
    pairs = [(rows_in, rows), (counts_in, counts)] + list(zip(refs[2:11], refs[14:23])) + [(refs[10], index)]
    copies = [pltpu.make_async_copy(a, b, sems.at[i]) for i, (a, b) in enumerate(pairs)]
    for copy in copies:
        copy.start()
    acc[...] = jnp.zeros_like(acc)
    padded[...] = jnp.zeros_like(padded)
    i = lax.broadcasted_iota(jnp.int32, (256, 256), 0)
    j = lax.broadcasted_iota(jnp.int32, (256, 256), 1)
    place = jnp.where(j < 128, j * 2, (j - 128) * 2 + 1)
    perm = jnp.where(i == place, 1.0, 0.0).astype(BF)
    copies[0].wait()
    copies[1].wait()
    slot = lax.broadcasted_iota(jnp.int32, (2, 128), 0)
    wanted = jnp.where(slot < counts[...], rows[...], 512)
    by_slot = jnp.concatenate([wanted[0:1, :], wanted[1:2, :]], axis=1)
    wide_rows = jnp.broadcast_to(by_slot, (128, 256))
    half = wide_rows // 2
    low = wide_rows - half * 2
    column = 2.0 * dot_nt(perm, half.astype(F32).astype(BF)) + dot_nt(perm, low.astype(F32).astype(BF))
    lane = lax.broadcasted_iota(jnp.int32, (256, 128), 1).astype(F32)
    for c in range(4):
        pick[:, c * 128 : (c + 1) * 128] = jnp.where(column == lane + 128.0 * c, 1.0, 0.0).astype(BF)
    copies[2].wait()
    send[:, 0:128] = dot(pick[...], feat[...]).astype(BF)
    copies[3].wait()
    padded[0:172, :] = grad_t[...]
    copies[4].wait()
    copies[11].wait()
    for b in range(4):
        part = padded[:, b * 128 : (b + 1) * 128]
        for k in range(3):
            e = index[k, 0, b]
            acc[e] += dot(part, tiles[b * 3 + k])
    for b in range(4):
        own_t[:, b * 128 : (b + 1) * 128] = acc[b]
    for b in range(2):
        send[b * 128 : (b + 1) * 128, 128:384] = acc[4 + b].T.astype(BF)
    for copy in copies[5:11]:
        copy.wait()


def gather_tiles(index, tiles, ext, b):
    total = dot(tiles[b * 3], ext[index[0, 0, b]])
    total += dot(tiles[b * 3 + 1], ext[index[1, 0, b]])
    total += dot(tiles[b * 3 + 2], ext[index[2, 0, b]])
    return total.astype(BF)


def middle_kernel(
    index, recv, feat, tiles, pick, own_t, grad_t, w1s, w1n, bias, w2s_t, w2n_t,
    hidden, project, out, ext, both, padded, wide_w, grads,
):
    for b in range(4):
        ext[b] = feat[b * 128 : (b + 1) * 128, :]
    for b in range(2):
        ext[4 + b] = recv[b * 128 : (b + 1) * 128, 0:128]
    both[:, 0:128] = feat[...]
    wide_w[...] = jnp.zeros_like(wide_w)
    for b in range(4):
        both[b * 128 : (b + 1) * 128, 128:256] = gather_tiles(index, tiles, ext, b)
    pre = dot(both[:, 0:128], w1s[...]) + dot(both[:, 128:256], w1n[...]) + bias[...]
    hid = jnp.maximum(pre, 0.0).astype(BF)
    hidden[...] = hid
    wide_w[256 : 256 + 172, :] = w2n_t[...]
    wide_w[256 + 192 : 256 + 236, :] = w2n_t[128:172, :]
    near = dot_nt(hid, wide_w[256:512, :]).astype(BF)
    project[...] = near
    picked = dot(pick[...], near).astype(BF)
    i = lax.broadcasted_iota(jnp.int32, (256, 256), 0)
    j = lax.broadcasted_iota(jnp.int32, (256, 256), 1)
    place_of = ((i >> 1) & 15) * 16 + (i >> 5) * 2 + (i & 1)
    heads = dot(jnp.where(j == place_of, 1.0, 0.0).astype(BF), picked[:, 0:128]).astype(BF)
    i = lax.broadcasted_iota(jnp.int32, (128, 256), 0)
    j = lax.broadcasted_iota(jnp.int32, (128, 256), 1)
    place_of = (i & 15) * 16 + (i >> 4) * 2
    tail0 = dot(jnp.where(j == place_of, 1.0, 0.0).astype(BF), picked[:, 128:256])
    tail1 = dot(jnp.where(j == place_of + 1, 1.0, 0.0).astype(BF), picked[:, 128:256])
    lane = lax.broadcasted_iota(jnp.int32, (128, 128), 1)
    tails = jnp.where(lane < 64, tail0, tail1).astype(BF)
    y = place()
    for p in range(8):
        out[p * 4 + y, 0:32, :] = heads[p * 32 : (p + 1) * 32, :]
        out[p * 4 + y, 32:48, :] = tails[p * 16 : (p + 1) * 16, :]
    padded[...] = jnp.zeros_like(padded)
    padded[0:172, :] = grad_t[...]
    wide_w[0:172, :] = w2s_t[...]
    returned_t = recv[:, 128:384].astype(F32).T.astype(BF)
    back_t = own_t[...] + dot(returned_t, pick[...])
    upper_t, lower_t = split(back_t)
    upper, lower = split(back_t.T)
    grad = padded[...]
    grad_hidden = dot(grad.astype(F32).T.astype(BF), wide_w[0:256, :])
    grad_hidden += dot(upper, wide_w[256:512, :]) + dot(lower, wide_w[256:512, :])
    grad_pre = jnp.where(pre > 0, grad_hidden, 0.0).astype(BF)
    first = dot(both[...].astype(F32).T.astype(BF), grad_pre)
    bias_sum = jnp.sum(grad_pre.astype(F32), axis=0, keepdims=True)
    self2 = dot(grad, hid)
    neigh2 = dot(upper_t, hid) + dot(lower_t, hid)
    row = lax.broadcasted_iota(jnp.int32, (176, 256), 0)
    self2 = jnp.where(row == 172, bias_sum, self2[0:176, :])
    neigh2 = neigh2[0:176, :]
    for h in range(2):
        cols = slice(h * 128, (h + 1) * 128)
        base = h * 640
        grads[base : base + 256, :] = first[:, cols].astype(BF)
        grads[base + 256 : base + 432, :] = self2[:, cols].astype(BF)
        grads[base + 432 : base + 608, :] = neigh2[:, cols].astype(BF)
        grads[base + 608 : base + 640, :] = jnp.zeros((32, 128), BF)
    for p in range(32):
        out[p, 48:88, :] = grads[p * 40 : (p + 1) * 40, :]


def plane_kernel(parts, out):
    total = parts[0, 48:88, :].astype(F32)
    for p in range(1, 32):
        total += parts[p, 48:88, :].astype(F32)
    total = total.astype(BF)
    y = place()
    i = lax.broadcasted_iota(jnp.int32, (256, 256), 0)
    j = lax.broadcasted_iota(jnp.int32, (256, 256), 1)
    place_of = ((i >> 1) & 7) * 32 + (i >> 4) * 2 + (i & 1)
    heads = jnp.concatenate([parts[p * 4 + y, 0:32, :] for p in range(8)], axis=0)
    heads = dot(jnp.where(j == place_of, 1.0, 0.0).astype(BF), heads).astype(BF)
    i = lax.broadcasted_iota(jnp.int32, (128, 128), 0)
    j = lax.broadcasted_iota(jnp.int32, (128, 128), 1)
    place_of = (i & 7) * 16 + (i >> 3)
    tails = jnp.concatenate([parts[p * 4 + y, 32:48, :] for p in range(8)], axis=0)
    tails = dot(jnp.where(j == place_of, 1.0, 0.0).astype(BF), tails).astype(BF)
    for z in range(16):
        out[z, 0:16, :] = heads[z * 16 : (z + 1) * 16, :]
        out[z, 16:24, :] = tails[z * 8 : (z + 1) * 8, :]
        out[z, 24:64, :] = total


def layer_kernel(parts, out):
    total = parts[0, 24:64, :].astype(F32)
    for p in range(1, 16):
        total += parts[p, 24:64, :].astype(F32)
    total = total.astype(BF)
    for p in range(32):
        out[p] = total


def logits_kernel(index, recv, hidden, project, tiles, w2s_t, out_t, ext, wide_w, result):
    for b in range(4):
        ext[b] = project[b * 128 : (b + 1) * 128, :]
    tails = jnp.concatenate([recv[z, 16:24, :] for z in range(16)], axis=0)
    i = lax.broadcasted_iota(jnp.int32, (256, 128), 0)
    j = lax.broadcasted_iota(jnp.int32, (256, 128), 1)
    tails = dot(jnp.where(j == (i >> 1), 1.0, 0.0).astype(BF), tails)
    m = lax.broadcasted_iota(jnp.int32, (128, 128), 0)
    n = lax.broadcasted_iota(jnp.int32, (128, 128), 1)
    other = dot(tails.astype(BF), jnp.where(n == (m ^ 64), 1.0, 0.0).astype(BF))
    tails = jnp.where((i & 1) == 0, tails, other).astype(BF)
    for z in range(16):
        ext[4 + z // 8, (z % 8) * 16 : (z % 8) * 16 + 16, 0:128] = recv[z, 0:16, :]
    for b in range(2):
        ext[4 + b, :, 128:256] = tails[b * 128 : (b + 1) * 128, :]
    wide_w[...] = jnp.zeros_like(wide_w)
    wide_w[0:172, :] = w2s_t[...]
    for b in range(4):
        rows = slice(b * 128, (b + 1) * 128)
        total = dot_nt(hidden[rows, :], wide_w[...])
        for k in range(3):
            total += dot(tiles[b * 3 + k], ext[index[k, 0, b]])
        result[:, rows] = total.T
    out_t[...] = result[0:172, :].astype(BF)


def finish_kernel(total, self1, neigh1, bias, self2_t, neigh2_t):
    for h in range(2):
        cols = slice(h * 128, (h + 1) * 128)
        base = h * 640
        self1[:, cols] = total[base : base + 128, :].astype(F32)
        neigh1[:, cols] = total[base + 128 : base + 256, :].astype(F32)
        self2 = total[base + 256 : base + 432, :].astype(F32)
        self2_t[:, cols] = self2[0:172, :]
        bias[:, cols] = self2[172:173, :]
        neigh2_t[:, cols] = total[base + 432 : base + 608, :].astype(F32)[0:172, :]


def shape(dims, dtype):
    return jax.ShapeDtypeStruct(dims, dtype)


def before(rows, counts, *kept):
    here = [pltpu.with_memory_space_constraint(value, pltpu.HBM) for value in (rows, counts) + kept]
    return pl.pallas_call(
        before_kernel,
        out_shape=(shape((256, 384), BF), shape((256, 512), BF), shape((256, 512), F32))
        + tuple(shape(value.shape, value.dtype) for value in kept),
        in_specs=[pl.BlockSpec(memory_space=pltpu.HBM)] * 11,
        out_specs=(VM,) * 12,
        scratch_shapes=[
            pltpu.VMEM((2, 128), jnp.int32),
            pltpu.VMEM((1, 128), jnp.int32),
            pltpu.SMEM((3, 1, 4), jnp.int32),
            pltpu.VMEM((6, 256, 128), F32),
            pltpu.VMEM((256, 512), BF),
            pltpu.SemaphoreType.DMA((12,)),
        ],
        compiler_params=PARAMS,
    )(*here)


def middle(index, recv, feat, tiles, pick, own_t, grad_t, w1s, w1n, bias, w2s_t, w2n_t):
    return pl.pallas_call(
        middle_kernel,
        out_shape=(shape((512, 256), BF), shape((512, 256), BF), shape((32, 88, 128), BF)),
        in_specs=[SM] + [VM] * 11,
        out_specs=(VM, VM, VM),
        scratch_shapes=[
            pltpu.VMEM((6, 128, 128), BF),
            pltpu.VMEM((512, 256), BF),
            pltpu.VMEM((256, 512), BF),
            pltpu.VMEM((512, 256), BF),
            pltpu.VMEM((1280, 128), BF),
        ],
        compiler_params=PARAMS,
    )(index, recv, feat, tiles, pick, own_t, grad_t, w1s, w1n, bias, w2s_t, w2n_t)


def scores(index, recv, hidden, project, tiles, w2s_t):
    return pl.pallas_call(
        logits_kernel,
        out_shape=shape((172, 512), BF),
        in_specs=[SM] + [VM] * 5,
        out_specs=VM,
        scratch_shapes=[
            pltpu.VMEM((6, 128, 256), BF),
            pltpu.VMEM((256, 256), BF),
            pltpu.VMEM((256, 512), F32),
        ],
        compiler_params=PARAMS,
    )(index, recv, hidden, project, tiles, w2s_t)


def after_plane(parts):
    return pl.pallas_call(
        plane_kernel,
        out_shape=shape((16, 64, 128), BF),
        in_specs=[VM],
        out_specs=VM,
        compiler_params=PARAMS,
    )(parts)


def after_layers(parts):
    return pl.pallas_call(
        layer_kernel,
        out_shape=shape((32, 40, 128), BF),
        in_specs=[VM],
        out_specs=VM,
        compiler_params=PARAMS,
    )(parts)


def finish(total):
    return pl.pallas_call(
        finish_kernel,
        out_shape=(
            shape((128, 256), F32),
            shape((128, 256), F32),
            shape((1, 256), F32),
            shape((172, 256), F32),
            shape((172, 256), F32),
        ),
        in_specs=[VM],
        out_specs=(VM,) * 5,
        compiler_params=PARAMS,
    )(total)


def exchange(values, axes):
    return lax.all_to_all(values, axes, split_axis=0, concat_axis=0, tiled=True)


def shards(
    features,
    send_rows,
    send_counts,
    tile_index,
    tile_weight,
    first_layer_self_weight,
    first_layer_neighbour_weight,
    layer1_bias,
    layer2_self,
    layer2_neigh,
    grad_logits,
):
    feat = features.reshape(512, 128)
    rows = jnp.swapaxes(send_rows.reshape(128, 2), 0, 1)
    counts = send_counts.reshape(1, 128)
    index = jnp.transpose(tile_index, (0, 3, 1, 2)).reshape(3, 1, 4)
    tiles = tile_weight.reshape(12, 128, 128)
    grad_t = jnp.swapaxes(grad_logits.reshape(512, 172), 0, 1)
    w2s_t = jnp.swapaxes(layer2_self, 0, 1)
    w2n_t = jnp.swapaxes(layer2_neigh, 0, 1)
    bias = layer1_bias.reshape(1, 256)

    send1, pick, own_t, feat, grad_t, tiles, w1s, w1n, bias, w2s_t, w2n_t, index = before(
        rows, counts, feat, grad_t, tiles,
        first_layer_self_weight, first_layer_neighbour_weight, bias, w2s_t, w2n_t, index,
    )
    recv1 = exchange(send1.reshape(128, 2, 384), WIDE).reshape(256, 384)
    hidden, project, parts = middle(
        index, recv1, feat, tiles, pick, own_t, grad_t,
        w1s, w1n, bias, w2s_t, w2n_t,
    )
    recv2 = exchange(after_plane(exchange(parts, PLANE)), "z")
    total = exchange(after_layers(recv2), PLANE)
    logits_t = scores(index, recv2, hidden, project, tiles, w2s_t)
    self1, neigh1, bias1, self2_t, neigh2_t = finish(total.reshape(1280, 128))
    logits = jnp.swapaxes(logits_t, 0, 1).reshape(1, 1, 512, 172)
    return (
        logits,
        self1,
        neigh1,
        bias1.reshape(256),
        jnp.swapaxes(self2_t, 0, 1),
        jnp.swapaxes(neigh2_t, 0, 1),
    )


def solution(mesh):
    fine = Mesh(mesh.devices.reshape(16, 4, 2, 4), ("z", "x", "core", "y"))
    return jax.shard_map(
        shards,
        mesh=fine,
        in_specs=(
            P(WIDE, "y", None, None),
            P(WIDE, "y", None, None),
            P(WIDE, "y", None),
            P(WIDE, "y", None, None),
            P(WIDE, "y", None, None, None, None),
            P(),
            P(),
            P(),
            P(),
            P(),
            P(WIDE, "y", None, None),
        ),
        out_specs=(P(WIDE, "y", None, None), P(), P(), P(), P(), P()),
        check_vma=False,
    )
```

```python
import jax
import jax.numpy as jnp
from jax import lax
from jax.experimental import pallas as pl
from jax.experimental.pallas import tpu as pltpu
from jax.sharding import Mesh, PartitionSpec as P

BF = jnp.bfloat16
F32 = jnp.float32
PLANE = ("x", "core", "y")
WIDE = ("z", "x", "core")
VM = pl.BlockSpec(memory_space=pltpu.VMEM)
SM = pl.BlockSpec(memory_space=pltpu.SMEM)
PARAMS = pltpu.CompilerParams(vmem_limit_bytes=32 * 1024 * 1024)


def dot(a, b):
    return jnp.dot(a, b, preferred_element_type=F32)


def dot_nt(a, b):
    return lax.dot_general(a, b, (((1,), (1,)), ((), ())), preferred_element_type=F32)


def split(values):
    upper = values.astype(BF)
    return upper, (values - upper.astype(F32)).astype(BF)


def place():
    return lax.axis_index("y")


def before_kernel(*refs):
    rows_in, counts_in = refs[0:2]
    send, pick, pick_out, own_t = refs[11:15]
    feat, grad_t, tiles = refs[15:18]
    rows, counts, index, acc, padded, sems = refs[24:30]
    pairs = [(rows_in, rows), (counts_in, counts)] + list(zip(refs[2:11], refs[15:24])) + [(refs[10], index)]
    copies = [pltpu.make_async_copy(a, b, sems.at[i]) for i, (a, b) in enumerate(pairs)]
    for copy in copies:
        copy.start()
    acc[...] = jnp.zeros_like(acc)
    padded[...] = jnp.zeros_like(padded)
    i = lax.broadcasted_iota(jnp.int32, (256, 256), 0)
    j = lax.broadcasted_iota(jnp.int32, (256, 256), 1)
    orders = (((i & 1) * 128 + (i >> 1), pick), (((i >> 4) & 1) * 128 + (i & 15) * 8 + (i >> 5), pick_out))
    copies[0].wait()
    copies[1].wait()
    slot = lax.broadcasted_iota(jnp.int32, (2, 128), 0)
    wanted = jnp.where(slot < counts[...], rows[...], 512)
    by_slot = jnp.concatenate([wanted[0:1, :], wanted[1:2, :]], axis=1)
    wide_rows = jnp.broadcast_to(by_slot, (128, 256))
    half = wide_rows // 2
    low = wide_rows - half * 2
    half = half.astype(F32).astype(BF)
    low = low.astype(F32).astype(BF)
    lane = lax.broadcasted_iota(jnp.int32, (256, 128), 1).astype(F32)
    for place_of, target in orders:
        perm = jnp.where(j == place_of, 1.0, 0.0).astype(BF)
        column = 2.0 * dot_nt(perm, half) + dot_nt(perm, low)
        if target is pick:
            live = jnp.where(column < 512.0, 1.0, 0.0)
        for c in range(4):
            target[:, c * 128 : (c + 1) * 128] = jnp.where(column == lane + 128.0 * c, 1.0, 0.0).astype(BF)
    copies[2].wait()
    send[:, 0:128] = dot(pick[...], feat[...]).astype(BF)
    copies[3].wait()
    padded[0:172, :] = grad_t[...]
    copies[4].wait()
    copies[11].wait()
    for b in range(4):
        part = padded[:, b * 128 : (b + 1) * 128]
        for k in range(3):
            e = index[k, 0, b]
            acc[e] += dot(part, tiles[b * 3 + k])
    for b in range(4):
        own_t[:, b * 128 : (b + 1) * 128] = acc[b]
    for b in range(2):
        rows_of = slice(b * 128, (b + 1) * 128)
        back = acc[4 + b].T
        tail = jnp.where(lane[rows_of, :] == 44.0, live[rows_of, :], back[:, 128:256])
        send[rows_of, 128:256] = back[:, 0:128].astype(BF)
        send[rows_of, 256:384] = tail.astype(BF)
    for copy in copies[5:11]:
        copy.wait()


def gather_tiles(index, tiles, ext, b):
    total = dot(tiles[b * 3], ext[index[0, 0, b]])
    total += dot(tiles[b * 3 + 1], ext[index[1, 0, b]])
    total += dot(tiles[b * 3 + 2], ext[index[2, 0, b]])
    return total.astype(BF)


def middle_kernel(
    index, recv, feat, tiles, pick, pick_out, own_t, grad_t, w1s, w1n, bias, w2s_t, w2n_t,
    hidden, out, ext, both, padded, wide_w,
):
    for b in range(4):
        ext[b] = feat[b * 128 : (b + 1) * 128, :]
    for b in range(2):
        ext[4 + b] = recv[b * 128 : (b + 1) * 128, 0:128]
    both[:, 0:128] = feat[...]
    wide_w[...] = jnp.zeros_like(wide_w)
    for b in range(4):
        both[b * 128 : (b + 1) * 128, 128:256] = gather_tiles(index, tiles, ext, b)
    picked = dot(pick_out[...], both[:, 128:256]).astype(BF)
    y = place()
    for p in range(8):
        out[p * 4 + y, 0:32, :] = picked[p * 32 : (p + 1) * 32, :]
    pre = dot(both[:, 0:128], w1s[...]) + dot(both[:, 128:256], w1n[...]) + bias[...]
    hid = jnp.maximum(pre, 0.0).astype(BF)
    hidden[...] = hid
    padded[...] = jnp.zeros_like(padded)
    padded[0:172, :] = grad_t[...]
    wide_w[0:172, :] = w2s_t[...]
    wide_w[256 : 256 + 172, :] = w2n_t[...]
    returned_t = recv[:, 128:384].astype(F32).T.astype(BF)
    back_t = own_t[...] + dot(returned_t, pick[...])
    upper_t, lower_t = split(back_t)
    upper, lower = split(back_t.T)
    grad = padded[...]
    grad_hidden = dot(grad.astype(F32).T.astype(BF), wide_w[0:256, :])
    grad_hidden += dot(upper, wide_w[256:512, :]) + dot(lower, wide_w[256:512, :])
    grad_pre = jnp.where(pre > 0, grad_hidden, 0.0).astype(BF)
    first = dot(both[...].astype(F32).T.astype(BF), grad_pre)
    bias_sum = jnp.sum(grad_pre.astype(F32), axis=0, keepdims=True)
    self2 = dot(grad, hid)
    neigh2 = dot(upper_t, hid) + dot(lower_t, hid)
    row = lax.broadcasted_iota(jnp.int32, (176, 256), 0)
    self2 = jnp.where(row == 172, bias_sum, self2[0:176, :])
    neigh2 = neigh2[0:176, :]
    rest = jnp.concatenate([self2, neigh2, jnp.zeros((32, 256), F32)], axis=0)
    grads = jnp.concatenate([first, rest], axis=0).astype(BF)
    for p in range(32):
        out[p, 32:72, :] = grads[(p % 16) * 40 : (p % 16) * 40 + 40, (p // 16) * 128 : (p // 16) * 128 + 128]


def plane_kernel(parts, out):
    total = parts[0, 32:72, :].astype(F32)
    for p in range(1, 32):
        total += parts[p, 32:72, :].astype(F32)
    total = total.astype(BF)
    y = place()
    i = lax.broadcasted_iota(jnp.int32, (256, 256), 0)
    j = lax.broadcasted_iota(jnp.int32, (256, 256), 1)
    place_of = ((i >> 1) & 7) * 32 + (i & 1) * 16 + (i >> 4)
    rows = jnp.concatenate([parts[p * 4 + y, 0:32, :] for p in range(8)], axis=0)
    rows = dot(jnp.where(j == place_of, 1.0, 0.0).astype(BF), rows).astype(BF)
    for z in range(16):
        out[z, 0:16, :] = rows[z * 16 : (z + 1) * 16, :]
        out[z, 16:56, :] = total


def layer_kernel(parts, out, four, sems):
    total = parts[0, 16:56, :].astype(F32)
    for p in range(1, 16):
        total += parts[p, 16:56, :].astype(F32)
    total = total.astype(BF)
    for p in range(4):
        four[p] = total
    copies = [pltpu.make_async_copy(four, out.at[p * 4 : p * 4 + 4], sems.at[p]) for p in range(8)]
    for copy in copies:
        copy.start()
    for copy in copies:
        copy.wait()


def logits_kernel(index, recv1, recv2, hidden, tiles, w1s, w1n, bias, w2s_t, w2n_t, out_t, ext, agg):
    far = jnp.concatenate([recv2[z, 0:16, :] for z in range(16)], axis=0)
    pre = dot(recv1[:, 0:128], w1s[...]) + dot(far, w1n[...]) + bias[...]
    i = lax.broadcasted_iota(jnp.int32, (128, 256), 0)
    live = dot(recv1[:, 256:384], jnp.where(i == 44, 1.0, 0.0).astype(BF))
    far = jnp.where(live > 0.5, jnp.maximum(pre, 0.0), 0.0).astype(BF)
    for b in range(4):
        ext[b] = hidden[b * 128 : (b + 1) * 128, :]
    for b in range(2):
        ext[4 + b] = far[b * 128 : (b + 1) * 128, :]
    for b in range(4):
        agg[b * 128 : (b + 1) * 128, :] = gather_tiles(index, tiles, ext, b)
    scores = dot_nt(w2s_t[...], hidden[...]) + dot_nt(w2n_t[...], agg[...])
    out_t[...] = scores.astype(BF)


def finish_kernel(total, self1, neigh1, bias, self2_t, neigh2_t):
    for h in range(2):
        cols = slice(h * 128, (h + 1) * 128)
        base = h * 640
        self1[:, cols] = total[base : base + 128, :].astype(F32)
        neigh1[:, cols] = total[base + 128 : base + 256, :].astype(F32)
        self2 = total[base + 256 : base + 432, :].astype(F32)
        self2_t[:, cols] = self2[0:172, :]
        bias[:, cols] = self2[172:173, :]
        neigh2_t[:, cols] = total[base + 432 : base + 608, :].astype(F32)[0:172, :]


def shape(dims, dtype):
    return jax.ShapeDtypeStruct(dims, dtype)


def before(rows, counts, *kept):
    here = [pltpu.with_memory_space_constraint(value, pltpu.HBM) for value in (rows, counts) + kept]
    return pl.pallas_call(
        before_kernel,
        out_shape=(shape((256, 384), BF), shape((256, 512), BF), shape((256, 512), BF), shape((256, 512), F32))
        + tuple(shape(value.shape, value.dtype) for value in kept),
        in_specs=[pl.BlockSpec(memory_space=pltpu.HBM)] * 11,
        out_specs=(VM,) * 13,
        scratch_shapes=[
            pltpu.VMEM((2, 128), jnp.int32),
            pltpu.VMEM((1, 128), jnp.int32),
            pltpu.SMEM((3, 1, 4), jnp.int32),
            pltpu.VMEM((6, 256, 128), F32),
            pltpu.VMEM((256, 512), BF),
            pltpu.SemaphoreType.DMA((12,)),
        ],
        compiler_params=PARAMS,
    )(*here)


def middle(index, recv, feat, tiles, pick, pick_out, own_t, grad_t, w1s, w1n, bias, w2s_t, w2n_t):
    return pl.pallas_call(
        middle_kernel,
        out_shape=(shape((512, 256), BF), shape((32, 72, 128), BF)),
        in_specs=[SM] + [VM] * 12,
        out_specs=(VM, VM),
        scratch_shapes=[
            pltpu.VMEM((6, 128, 128), BF),
            pltpu.VMEM((512, 256), BF),
            pltpu.VMEM((256, 512), BF),
            pltpu.VMEM((512, 256), BF),
        ],
        compiler_params=PARAMS,
    )(index, recv, feat, tiles, pick, pick_out, own_t, grad_t, w1s, w1n, bias, w2s_t, w2n_t)


def scores(index, recv1, recv2, hidden, tiles, w1s, w1n, bias, w2s_t, w2n_t):
    return pl.pallas_call(
        logits_kernel,
        out_shape=shape((172, 512), BF),
        in_specs=[SM] + [VM] * 9,
        out_specs=VM,
        scratch_shapes=[pltpu.VMEM((6, 128, 256), BF), pltpu.VMEM((512, 256), BF)],
        compiler_params=PARAMS,
    )(index, recv1, recv2, hidden, tiles, w1s, w1n, bias, w2s_t, w2n_t)


def after_plane(parts):
    return pl.pallas_call(
        plane_kernel,
        out_shape=shape((16, 56, 128), BF),
        in_specs=[VM],
        out_specs=VM,
        compiler_params=PARAMS,
    )(parts)


def after_layers(parts):
    return pl.pallas_call(
        layer_kernel,
        out_shape=shape((32, 40, 128), BF),
        in_specs=[VM],
        out_specs=pl.BlockSpec(memory_space=pltpu.HBM),
        scratch_shapes=[pltpu.VMEM((4, 40, 128), BF), pltpu.SemaphoreType.DMA((8,))],
        compiler_params=PARAMS,
    )(parts)


def finish(total):
    return pl.pallas_call(
        finish_kernel,
        out_shape=(
            shape((128, 256), F32),
            shape((128, 256), F32),
            shape((1, 256), F32),
            shape((172, 256), F32),
            shape((172, 256), F32),
        ),
        in_specs=[VM],
        out_specs=(VM,) * 5,
        compiler_params=PARAMS,
    )(total)


def exchange(values, axes):
    return lax.all_to_all(values, axes, split_axis=0, concat_axis=0, tiled=True)


def shards(
    features,
    send_rows,
    send_counts,
    tile_index,
    tile_weight,
    first_layer_self_weight,
    first_layer_neighbour_weight,
    layer1_bias,
    layer2_self,
    layer2_neigh,
    grad_logits,
):
    feat = features.reshape(512, 128)
    rows = jnp.swapaxes(send_rows.reshape(128, 2), 0, 1)
    counts = send_counts.reshape(1, 128)
    index = jnp.transpose(tile_index, (0, 3, 1, 2)).reshape(3, 1, 4)
    tiles = tile_weight.reshape(12, 128, 128)
    grad_t = jnp.swapaxes(grad_logits.reshape(512, 172), 0, 1)
    w2s_t = jnp.swapaxes(layer2_self, 0, 1)
    w2n_t = jnp.swapaxes(layer2_neigh, 0, 1)
    bias = layer1_bias.reshape(1, 256)

    send1, pick, pick_out, own_t, feat, grad_t, tiles, w1s, w1n, bias, w2s_t, w2n_t, index = before(
        rows, counts, feat, grad_t, tiles,
        first_layer_self_weight, first_layer_neighbour_weight, bias, w2s_t, w2n_t, index,
    )
    recv1 = exchange(send1.reshape(128, 2, 384), WIDE).reshape(256, 384)
    hidden, parts = middle(
        index, recv1, feat, tiles, pick, pick_out, own_t, grad_t,
        w1s, w1n, bias, w2s_t, w2n_t,
    )
    recv2 = exchange(after_plane(exchange(parts, PLANE)), "z")
    total = exchange(after_layers(recv2), PLANE)
    logits_t = scores(index, recv1, recv2, hidden, tiles, w1s, w1n, bias, w2s_t, w2n_t)
    self1, neigh1, bias1, self2_t, neigh2_t = finish(total.reshape(1280, 128))
    logits = jnp.swapaxes(logits_t, 0, 1).reshape(1, 1, 512, 172)
    return (
        logits,
        self1,
        neigh1,
        bias1.reshape(256),
        jnp.swapaxes(self2_t, 0, 1),
        jnp.swapaxes(neigh2_t, 0, 1),
    )


def solution(mesh):
    fine = Mesh(mesh.devices.reshape(16, 4, 2, 4), ("z", "x", "core", "y"))
    return jax.shard_map(
        shards,
        mesh=fine,
        in_specs=(
            P(WIDE, "y", None, None),
            P(WIDE, "y", None, None),
            P(WIDE, "y", None),
            P(WIDE, "y", None, None),
            P(WIDE, "y", None, None, None, None),
            P(),
            P(),
            P(),
            P(),
            P(),
            P(WIDE, "y", None, None),
        ),
        out_specs=(P(WIDE, "y", None, None), P(), P(), P(), P(), P()),
        check_vma=False,
    )
```

```python
import jax
import jax.numpy as jnp
from jax import lax
from jax.experimental import pallas as pl
from jax.experimental.pallas import tpu as pltpu
from jax.sharding import Mesh, PartitionSpec as P

BF = jnp.bfloat16
F32 = jnp.float32
PLANE = ("x", "core", "y")
WIDE = ("z", "x", "core")
VM = pl.BlockSpec(memory_space=pltpu.VMEM)
SM = pl.BlockSpec(memory_space=pltpu.SMEM)
PARAMS = pltpu.CompilerParams(vmem_limit_bytes=32 * 1024 * 1024)


def dot(a, b):
    return jnp.dot(a, b, preferred_element_type=F32)


def dot_nt(a, b):
    return lax.dot_general(a, b, (((1,), (1,)), ((), ())), preferred_element_type=F32)


def dot_tn(a, b):
    return lax.dot_general(a, b, (((0,), (0,)), ((), ())), preferred_element_type=F32)


def place():
    return lax.axis_index("y")


def before_kernel(*refs):
    rows_in, counts_in = refs[0:2]
    send, pick, pick_out, own_t = refs[11:15]
    feat, grad_t, tiles = refs[15:18]
    rows, counts, index, acc, padded, sems = refs[24:30]
    pairs = [(rows_in, rows), (counts_in, counts)] + list(zip(refs[2:11], refs[15:24])) + [(refs[10], index)]
    copies = [pltpu.make_async_copy(a, b, sems.at[i]) for i, (a, b) in enumerate(pairs)]
    for copy in copies:
        copy.start()
    acc[...] = jnp.zeros_like(acc)
    padded[...] = jnp.zeros_like(padded)
    i = lax.broadcasted_iota(jnp.int32, (256, 256), 0)
    j = lax.broadcasted_iota(jnp.int32, (256, 256), 1)
    orders = (((i & 1) * 128 + (i >> 1), pick), (((i >> 4) & 1) * 128 + (i & 15) * 8 + (i >> 5), pick_out))
    copies[0].wait()
    copies[1].wait()
    slot = lax.broadcasted_iota(jnp.int32, (2, 128), 0)
    wanted = jnp.where(slot < counts[...], rows[...], 512)
    by_slot = jnp.concatenate([wanted[0:1, :], wanted[1:2, :]], axis=1)
    wide_rows = jnp.broadcast_to(by_slot, (128, 256))
    half = wide_rows // 2
    low = wide_rows - half * 2
    half = half.astype(F32).astype(BF)
    low = low.astype(F32).astype(BF)
    lane = lax.broadcasted_iota(jnp.int32, (256, 128), 1).astype(F32)
    for place_of, target in orders:
        perm = jnp.where(j == place_of, 1.0, 0.0).astype(BF)
        column = 2.0 * dot_nt(perm, half) + dot_nt(perm, low)
        if target is pick:
            live = jnp.where(column < 512.0, 1.0, 0.0)
        for c in range(4):
            target[:, c * 128 : (c + 1) * 128] = jnp.where(column == lane + 128.0 * c, 1.0, 0.0).astype(BF)
    copies[2].wait()
    send[:, 0:128] = dot(pick[...], feat[...]).astype(BF)
    copies[3].wait()
    padded[0:172, :] = grad_t[...]
    copies[4].wait()
    copies[11].wait()
    for b in range(4):
        part = padded[:, b * 128 : (b + 1) * 128]
        for k in range(3):
            e = index[k, 0, b]
            acc[e] += dot(part, tiles[b * 3 + k])
    for b in range(4):
        own_t[:, b * 128 : (b + 1) * 128] = acc[b]
    for b in range(2):
        rows_of = slice(b * 128, (b + 1) * 128)
        back = acc[4 + b].T
        tail = jnp.where(lane[rows_of, :] == 44.0, live[rows_of, :], back[:, 128:256])
        send[rows_of, 128:256] = back[:, 0:128].astype(BF)
        send[rows_of, 256:384] = tail.astype(BF)
    for copy in copies[5:11]:
        copy.wait()


def gather_tiles(index, tiles, ext, b):
    total = dot(tiles[b * 3], ext[index[0, 0, b]])
    total += dot(tiles[b * 3 + 1], ext[index[1, 0, b]])
    total += dot(tiles[b * 3 + 2], ext[index[2, 0, b]])
    return total.astype(BF)


def middle_kernel(
    index, recv, feat, tiles, pick, pick_out, own_t, grad_t, w1s, w1n, bias, w2s_t, w2n_t,
    hidden, out, ext, both, padded, wide_w,
):
    for b in range(4):
        ext[b] = feat[b * 128 : (b + 1) * 128, :]
    for b in range(2):
        ext[4 + b] = recv[b * 128 : (b + 1) * 128, 0:128]
    both[:, 0:128] = feat[...]
    wide_w[...] = jnp.zeros_like(wide_w)
    for b in range(4):
        both[b * 128 : (b + 1) * 128, 128:256] = gather_tiles(index, tiles, ext, b)
    picked = dot(pick_out[...], both[:, 128:256]).astype(BF)
    y = place()
    for p in range(8):
        out[p * 4 + y, 0:32, :] = picked[p * 32 : (p + 1) * 32, :]
    pre = dot(both[:, 0:128], w1s[...]) + dot(both[:, 128:256], w1n[...]) + bias[...]
    hid = jnp.maximum(pre, 0.0).astype(BF)
    hidden[...] = hid
    padded[...] = jnp.zeros_like(padded)
    padded[0:172, :] = grad_t[...]
    wide_w[0:172, :] = w2s_t[...]
    wide_w[256 : 256 + 172, :] = w2n_t[...]
    returned_t = recv[:, 128:384].astype(F32).T.astype(BF)
    back_t = own_t[...] + dot(returned_t, pick[...])
    upper_t = back_t.astype(BF)
    grad = padded[...]
    grad_hidden = dot_tn(jnp.concatenate([grad, upper_t], axis=0), wide_w[...])
    grad_pre = jnp.where(pre > 0, grad_hidden, 0.0).astype(BF)
    first = dot(both[...].astype(F32).T.astype(BF), grad_pre)
    bias_sum = jnp.sum(grad_pre.astype(F32), axis=0, keepdims=True)
    self2 = dot(grad, hid)
    neigh2 = dot(upper_t, hid)
    row = lax.broadcasted_iota(jnp.int32, (176, 256), 0)
    self2 = jnp.where(row == 172, bias_sum, self2[0:176, :])
    neigh2 = neigh2[0:176, :]
    rest = jnp.concatenate([self2, neigh2, jnp.zeros((32, 256), F32)], axis=0)
    grads = jnp.concatenate([first, rest], axis=0).astype(BF)
    for p in range(32):
        out[p, 32:72, :] = grads[(p % 16) * 40 : (p % 16) * 40 + 40, (p // 16) * 128 : (p // 16) * 128 + 128]


def plane_kernel(parts, out):
    total = parts[0, 32:72, :].astype(F32)
    for p in range(1, 32):
        total += parts[p, 32:72, :].astype(F32)
    total = total.astype(BF)
    y = place()
    i = lax.broadcasted_iota(jnp.int32, (256, 256), 0)
    j = lax.broadcasted_iota(jnp.int32, (256, 256), 1)
    place_of = ((i >> 1) & 7) * 32 + (i & 1) * 16 + (i >> 4)
    rows = jnp.concatenate([parts[p * 4 + y, 0:32, :] for p in range(8)], axis=0)
    rows = dot(jnp.where(j == place_of, 1.0, 0.0).astype(BF), rows).astype(BF)
    for z in range(16):
        out[z, 0:16, :] = rows[z * 16 : (z + 1) * 16, :]
        out[z, 16:56, :] = total


def layer_kernel(parts, out, four, sems):
    total = parts[0, 16:56, :].astype(F32)
    for p in range(1, 16):
        total += parts[p, 16:56, :].astype(F32)
    total = total.astype(BF)
    for p in range(4):
        four[p] = total
    copies = [pltpu.make_async_copy(four, out.at[p * 4 : p * 4 + 4], sems.at[p]) for p in range(8)]
    for copy in copies:
        copy.start()
    for copy in copies:
        copy.wait()


def logits_kernel(index, recv1, recv2, hidden, tiles, w1s, w1n, bias, w2s_t, w2n_t, out_t, ext, agg):
    far = jnp.concatenate([recv2[z, 0:16, :] for z in range(16)], axis=0)
    pre = dot(recv1[:, 0:128], w1s[...]) + dot(far, w1n[...]) + bias[...]
    i = lax.broadcasted_iota(jnp.int32, (128, 256), 0)
    live = dot(recv1[:, 256:384], jnp.where(i == 44, 1.0, 0.0).astype(BF))
    far = jnp.where(live > 0.5, jnp.maximum(pre, 0.0), 0.0).astype(BF)
    for b in range(4):
        ext[b] = hidden[b * 128 : (b + 1) * 128, :]
    for b in range(2):
        ext[4 + b] = far[b * 128 : (b + 1) * 128, :]
    for b in range(4):
        agg[b * 128 : (b + 1) * 128, :] = gather_tiles(index, tiles, ext, b)
    scores = dot_nt(w2s_t[...], hidden[...]) + dot_nt(w2n_t[...], agg[...])
    out_t[...] = scores.astype(BF)


def finish_kernel(total, self1, neigh1, bias, self2_t, neigh2_t):
    for h in range(2):
        cols = slice(h * 128, (h + 1) * 128)
        base = h * 640
        self1[:, cols] = total[base : base + 128, :].astype(F32)
        neigh1[:, cols] = total[base + 128 : base + 256, :].astype(F32)
        self2 = total[base + 256 : base + 432, :].astype(F32)
        self2_t[:, cols] = self2[0:172, :]
        bias[:, cols] = self2[172:173, :]
        neigh2_t[:, cols] = total[base + 432 : base + 608, :].astype(F32)[0:172, :]


def shape(dims, dtype):
    return jax.ShapeDtypeStruct(dims, dtype)


def before(rows, counts, *kept):
    here = [pltpu.with_memory_space_constraint(value, pltpu.HBM) for value in (rows, counts) + kept]
    return pl.pallas_call(
        before_kernel,
        out_shape=(shape((256, 384), BF), shape((256, 512), BF), shape((256, 512), BF), shape((256, 512), F32))
        + tuple(shape(value.shape, value.dtype) for value in kept),
        in_specs=[pl.BlockSpec(memory_space=pltpu.HBM)] * 11,
        out_specs=(VM,) * 13,
        scratch_shapes=[
            pltpu.VMEM((2, 128), jnp.int32),
            pltpu.VMEM((1, 128), jnp.int32),
            pltpu.SMEM((3, 1, 4), jnp.int32),
            pltpu.VMEM((6, 256, 128), F32),
            pltpu.VMEM((256, 512), BF),
            pltpu.SemaphoreType.DMA((12,)),
        ],
        compiler_params=PARAMS,
    )(*here)


def middle(index, recv, feat, tiles, pick, pick_out, own_t, grad_t, w1s, w1n, bias, w2s_t, w2n_t):
    return pl.pallas_call(
        middle_kernel,
        out_shape=(shape((512, 256), BF), shape((32, 72, 128), BF)),
        in_specs=[SM] + [VM] * 12,
        out_specs=(VM, VM),
        scratch_shapes=[
            pltpu.VMEM((6, 128, 128), BF),
            pltpu.VMEM((512, 256), BF),
            pltpu.VMEM((256, 512), BF),
            pltpu.VMEM((512, 256), BF),
        ],
        compiler_params=PARAMS,
    )(index, recv, feat, tiles, pick, pick_out, own_t, grad_t, w1s, w1n, bias, w2s_t, w2n_t)


def scores(index, recv1, recv2, hidden, tiles, w1s, w1n, bias, w2s_t, w2n_t):
    return pl.pallas_call(
        logits_kernel,
        out_shape=shape((172, 512), BF),
        in_specs=[SM] + [VM] * 9,
        out_specs=VM,
        scratch_shapes=[pltpu.VMEM((6, 128, 256), BF), pltpu.VMEM((512, 256), BF)],
        compiler_params=PARAMS,
    )(index, recv1, recv2, hidden, tiles, w1s, w1n, bias, w2s_t, w2n_t)


def after_plane(parts):
    return pl.pallas_call(
        plane_kernel,
        out_shape=shape((16, 56, 128), BF),
        in_specs=[VM],
        out_specs=VM,
        compiler_params=PARAMS,
    )(parts)


def after_layers(parts):
    return pl.pallas_call(
        layer_kernel,
        out_shape=shape((32, 40, 128), BF),
        in_specs=[VM],
        out_specs=pl.BlockSpec(memory_space=pltpu.HBM),
        scratch_shapes=[pltpu.VMEM((4, 40, 128), BF), pltpu.SemaphoreType.DMA((8,))],
        compiler_params=PARAMS,
    )(parts)


def finish(total):
    return pl.pallas_call(
        finish_kernel,
        out_shape=(
            shape((128, 256), F32),
            shape((128, 256), F32),
            shape((1, 256), F32),
            shape((172, 256), F32),
            shape((172, 256), F32),
        ),
        in_specs=[VM],
        out_specs=(VM,) * 5,
        compiler_params=PARAMS,
    )(total)


def exchange(values, axes):
    return lax.all_to_all(values, axes, split_axis=0, concat_axis=0, tiled=True)


def shards(
    features,
    send_rows,
    send_counts,
    tile_index,
    tile_weight,
    first_layer_self_weight,
    first_layer_neighbour_weight,
    layer1_bias,
    layer2_self,
    layer2_neigh,
    grad_logits,
):
    feat = features.reshape(512, 128)
    rows = jnp.swapaxes(send_rows.reshape(128, 2), 0, 1)
    counts = send_counts.reshape(1, 128)
    index = jnp.transpose(tile_index, (0, 3, 1, 2)).reshape(3, 1, 4)
    tiles = tile_weight.reshape(12, 128, 128)
    grad_t = jnp.swapaxes(grad_logits.reshape(512, 172), 0, 1)
    w2s_t = jnp.swapaxes(layer2_self, 0, 1)
    w2n_t = jnp.swapaxes(layer2_neigh, 0, 1)
    bias = layer1_bias.reshape(1, 256)

    send1, pick, pick_out, own_t, feat, grad_t, tiles, w1s, w1n, bias, w2s_t, w2n_t, index = before(
        rows, counts, feat, grad_t, tiles,
        first_layer_self_weight, first_layer_neighbour_weight, bias, w2s_t, w2n_t, index,
    )
    recv1 = exchange(send1.reshape(128, 2, 384), WIDE).reshape(256, 384)
    hidden, parts = middle(
        index, recv1, feat, tiles, pick, pick_out, own_t, grad_t,
        w1s, w1n, bias, w2s_t, w2n_t,
    )
    recv2 = exchange(after_plane(exchange(parts, PLANE)), "z")
    total = exchange(after_layers(recv2), PLANE)
    logits_t = scores(index, recv1, recv2, hidden, tiles, w1s, w1n, bias, w2s_t, w2n_t)
    self1, neigh1, bias1, self2_t, neigh2_t = finish(total.reshape(1280, 128))
    logits = jnp.swapaxes(logits_t, 0, 1).reshape(1, 1, 512, 172)
    return (
        logits,
        self1,
        neigh1,
        bias1.reshape(256),
        jnp.swapaxes(self2_t, 0, 1),
        jnp.swapaxes(neigh2_t, 0, 1),
    )


def solution(mesh):
    fine = Mesh(mesh.devices.reshape(16, 4, 2, 4), ("z", "x", "core", "y"))
    return jax.shard_map(
        shards,
        mesh=fine,
        in_specs=(
            P(WIDE, "y", None, None),
            P(WIDE, "y", None, None),
            P(WIDE, "y", None),
            P(WIDE, "y", None, None),
            P(WIDE, "y", None, None, None, None),
            P(),
            P(),
            P(),
            P(),
            P(),
            P(WIDE, "y", None, None),
        ),
        out_specs=(P(WIDE, "y", None, None), P(), P(), P(), P(), P()),
        check_vma=False,
    )
```

```python
import jax
import jax.numpy as jnp
from jax import lax
from jax.experimental import pallas as pl
from jax.experimental.pallas import tpu as pltpu
from jax.sharding import Mesh, PartitionSpec as P

BF = jnp.bfloat16
F32 = jnp.float32
PLANE = ("x", "core", "y")
WIDE = ("z", "x", "core")
VM = pl.BlockSpec(memory_space=pltpu.VMEM)
SM = pl.BlockSpec(memory_space=pltpu.SMEM)
PARAMS = pltpu.CompilerParams(vmem_limit_bytes=32 * 1024 * 1024)


def dot(a, b):
    return jnp.dot(a, b, preferred_element_type=F32)


def dot_nt(a, b):
    return lax.dot_general(a, b, (((1,), (1,)), ((), ())), preferred_element_type=F32)


def dot_tn(a, b):
    return lax.dot_general(a, b, (((0,), (0,)), ((), ())), preferred_element_type=F32)


def place():
    return lax.axis_index("y")


def before_kernel(*refs):
    rows_in, counts_in = refs[0:2]
    send, pick, pick_out, own_t = refs[11:15]
    feat, grad_t, tiles = refs[15:18]
    rows, counts, index, acc, padded, sems = refs[24:30]
    pairs = [(rows_in, rows), (counts_in, counts)] + list(zip(refs[2:11], refs[15:24])) + [(refs[10], index)]
    copies = [pltpu.make_async_copy(a, b, sems.at[i]) for i, (a, b) in enumerate(pairs)]
    for copy in copies:
        copy.start()
    acc[...] = jnp.zeros_like(acc)
    padded[...] = jnp.zeros_like(padded)
    i = lax.broadcasted_iota(jnp.int32, (256, 256), 0)
    j = lax.broadcasted_iota(jnp.int32, (256, 256), 1)
    orders = (((i & 1) * 128 + (i >> 1), pick), (((i >> 4) & 1) * 128 + (i & 15) * 8 + (i >> 5), pick_out))
    copies[0].wait()
    copies[1].wait()
    slot = lax.broadcasted_iota(jnp.int32, (2, 128), 0)
    wanted = jnp.where(slot < counts[...], rows[...], 512)
    by_slot = jnp.concatenate([wanted[0:1, :], wanted[1:2, :]], axis=1)
    wide_rows = jnp.broadcast_to(by_slot, (128, 256))
    half = wide_rows // 2
    low = wide_rows - half * 2
    half = half.astype(F32).astype(BF)
    low = low.astype(F32).astype(BF)
    lane = lax.broadcasted_iota(jnp.int32, (256, 128), 1).astype(F32)
    for place_of, target in orders:
        perm = jnp.where(j == place_of, 1.0, 0.0).astype(BF)
        column = 2.0 * dot_nt(perm, half) + dot_nt(perm, low)
        if target is pick:
            live = jnp.where(column < 512.0, 1.0, 0.0)
        for c in range(4):
            target[:, c * 128 : (c + 1) * 128] = jnp.where(column == lane + 128.0 * c, 1.0, 0.0).astype(BF)
    copies[2].wait()
    send[:, 0:128] = dot(pick[...], feat[...]).astype(BF)
    copies[3].wait()
    padded[0:172, :] = grad_t[...]
    copies[4].wait()
    copies[11].wait()
    for b in range(4):
        part = padded[:, b * 128 : (b + 1) * 128]
        for k in range(3):
            e = index[k, 0, b]
            acc[e] += dot(part, tiles[b * 3 + k])
    for b in range(4):
        own_t[:, b * 128 : (b + 1) * 128] = acc[b]
    for b in range(2):
        rows_of = slice(b * 128, (b + 1) * 128)
        back = acc[4 + b].T
        tail = jnp.where(lane[rows_of, :] == 44.0, live[rows_of, :], back[:, 128:256])
        send[rows_of, 128:256] = back[:, 0:128].astype(BF)
        send[rows_of, 256:384] = tail.astype(BF)
    for copy in copies[5:11]:
        copy.wait()


def gather_tiles(index, tiles, ext, b):
    total = dot(tiles[b * 3], ext[index[0, 0, b]])
    total += dot(tiles[b * 3 + 1], ext[index[1, 0, b]])
    total += dot(tiles[b * 3 + 2], ext[index[2, 0, b]])
    return total.astype(BF)


def middle_kernel(
    index_in, recv, feat, tiles, pick, pick_out, own_t, grad_t, w1s, w1n, bias, w2s_t, w2n_t,
    hidden, out, ext, both, padded, wide_w, index, sem,
):
    copy = pltpu.make_async_copy(index_in, index, sem)
    copy.start()
    for b in range(4):
        ext[b] = feat[b * 128 : (b + 1) * 128, :]
    for b in range(2):
        ext[4 + b] = recv[b * 128 : (b + 1) * 128, 0:128]
    both[:, 0:128] = feat[...]
    wide_w[...] = jnp.zeros_like(wide_w)
    padded[...] = jnp.zeros_like(padded)
    padded[0:172, :] = grad_t[...]
    wide_w[0:172, :] = w2s_t[...]
    wide_w[256 : 256 + 172, :] = w2n_t[...]
    returned_t = recv[:, 128:384].astype(F32).T.astype(BF)
    back_t = own_t[...] + dot(returned_t, pick[...])
    copy.wait()
    upper_t = back_t.astype(BF)
    grad = padded[...]
    grad_hidden = dot_tn(jnp.concatenate([grad, upper_t], axis=0), wide_w[...])
    for b in range(4):
        both[b * 128 : (b + 1) * 128, 128:256] = gather_tiles(index, tiles, ext, b)
    picked = dot(pick_out[...], both[:, 128:256]).astype(BF)
    y = place()
    for p in range(8):
        out[p * 4 + y, 0:32, :] = picked[p * 32 : (p + 1) * 32, :]
    pre = dot(both[:, 0:128], w1s[...]) + dot(both[:, 128:256], w1n[...]) + bias[...]
    hid = jnp.maximum(pre, 0.0).astype(BF)
    hidden[...] = hid
    grad_pre = jnp.where(pre > 0, grad_hidden, 0.0).astype(BF)
    first = dot(both[...].astype(F32).T.astype(BF), grad_pre)
    bias_sum = jnp.sum(grad_pre.astype(F32), axis=0, keepdims=True)
    self2 = dot(grad, hid)
    neigh2 = dot(upper_t, hid)
    row = lax.broadcasted_iota(jnp.int32, (176, 256), 0)
    self2 = jnp.where(row == 172, bias_sum, self2[0:176, :])
    neigh2 = neigh2[0:176, :]
    rest = jnp.concatenate([self2, neigh2, jnp.zeros((32, 256), F32)], axis=0)
    grads = jnp.concatenate([first, rest], axis=0).astype(BF)
    for p in range(32):
        out[p, 32:72, :] = grads[(p % 16) * 40 : (p % 16) * 40 + 40, (p // 16) * 128 : (p // 16) * 128 + 128]


def plane_kernel(parts, out):
    total = parts[0, 32:72, :].astype(F32)
    for p in range(1, 32):
        total += parts[p, 32:72, :].astype(F32)
    total = total.astype(BF)
    y = place()
    i = lax.broadcasted_iota(jnp.int32, (256, 256), 0)
    j = lax.broadcasted_iota(jnp.int32, (256, 256), 1)
    place_of = ((i >> 1) & 7) * 32 + (i & 1) * 16 + (i >> 4)
    rows = jnp.concatenate([parts[p * 4 + y, 0:32, :] for p in range(8)], axis=0)
    rows = dot(jnp.where(j == place_of, 1.0, 0.0).astype(BF), rows).astype(BF)
    for z in range(16):
        out[z, 0:16, :] = rows[z * 16 : (z + 1) * 16, :]
        out[z, 16:56, :] = total


def layer_kernel(parts, out):
    total = parts[0, 16:56, :].astype(F32)
    for p in range(1, 16):
        total += parts[p, 16:56, :].astype(F32)
    total = total.astype(BF)
    for p in range(32):
        out[p] = total


def last_kernel(
    index_in, total, recv1, recv2, hidden, tiles, w1s, w1n, bias, w2s_t, w2n_t,
    logits_out, self1_out, neigh1_out, bias_out, self2_out, neigh2_out,
    logits, self1, neigh1, bias1, self2_t, neigh2_t, ext, agg, sems, index, index_sem,
):
    copies = []
    fetch = pltpu.make_async_copy(index_in, index, index_sem)
    fetch.start()

    def leave(value, target):
        copies.append(pltpu.make_async_copy(value, target, sems.at[len(copies)]))
        copies[-1].start()

    def both(first, rows):
        halves = [total[base + first : base + first + rows, :].astype(F32) for base in (0, 640)]
        return jnp.concatenate(halves, axis=1)

    self1[...] = both(0, 128)
    leave(self1, self1_out)
    neigh1[...] = both(128, 128)
    leave(neigh1, neigh1_out)
    value = both(256, 176)
    self2_t[...] = value[0:172, :]
    leave(self2_t, self2_out)
    bias1[...] = value[172:173, :]
    leave(bias1, bias_out)
    neigh2_t[...] = both(432, 176)[0:172, :]
    leave(neigh2_t, neigh2_out)
    far = jnp.concatenate([recv2[z, 0:16, :] for z in range(16)], axis=0)
    pre = dot(recv1[:, 0:128], w1s[...]) + dot(far, w1n[...]) + bias[...]
    i = lax.broadcasted_iota(jnp.int32, (128, 256), 0)
    live = dot(recv1[:, 256:384], jnp.where(i == 44, 1.0, 0.0).astype(BF))
    far = jnp.where(live > 0.5, jnp.maximum(pre, 0.0), 0.0).astype(BF)
    for b in range(4):
        ext[b] = hidden[b * 128 : (b + 1) * 128, :]
    for b in range(2):
        ext[4 + b] = far[b * 128 : (b + 1) * 128, :]
    scores = dot_nt(w2s_t[...], hidden[...])
    fetch.wait()
    for b in range(4):
        agg[b * 128 : (b + 1) * 128, :] = gather_tiles(index, tiles, ext, b)
    scores += dot_nt(w2n_t[...], agg[...])
    logits[...] = scores.astype(BF)
    leave(logits, logits_out)
    for copy in copies:
        copy.wait()


def shape(dims, dtype):
    return jax.ShapeDtypeStruct(dims, dtype)


def before(rows, counts, *kept):
    here = [pltpu.with_memory_space_constraint(value, pltpu.HBM) for value in (rows, counts) + kept]
    return pl.pallas_call(
        before_kernel,
        out_shape=(shape((256, 384), BF), shape((256, 512), BF), shape((256, 512), BF), shape((256, 512), F32))
        + tuple(shape(value.shape, value.dtype) for value in kept),
        in_specs=[pl.BlockSpec(memory_space=pltpu.HBM)] * 11,
        out_specs=(VM,) * 13,
        scratch_shapes=[
            pltpu.VMEM((2, 128), jnp.int32),
            pltpu.VMEM((1, 128), jnp.int32),
            pltpu.SMEM((3, 1, 4), jnp.int32),
            pltpu.VMEM((6, 256, 128), F32),
            pltpu.VMEM((256, 512), BF),
            pltpu.SemaphoreType.DMA((12,)),
        ],
        compiler_params=PARAMS,
    )(*here)


def middle(index, recv, feat, tiles, pick, pick_out, own_t, grad_t, w1s, w1n, bias, w2s_t, w2n_t):
    return pl.pallas_call(
        middle_kernel,
        out_shape=(shape((512, 256), BF), shape((32, 72, 128), BF)),
        in_specs=[VM] * 13,
        out_specs=(VM, VM),
        scratch_shapes=[
            pltpu.VMEM((6, 128, 128), BF),
            pltpu.VMEM((512, 256), BF),
            pltpu.VMEM((256, 512), BF),
            pltpu.VMEM((512, 256), BF),
            pltpu.SMEM((3, 1, 4), jnp.int32),
            pltpu.SemaphoreType.DMA,
        ],
        compiler_params=PARAMS,
    )(index, recv, feat, tiles, pick, pick_out, own_t, grad_t, w1s, w1n, bias, w2s_t, w2n_t)


def after_plane(parts):
    return pl.pallas_call(
        plane_kernel,
        out_shape=shape((16, 56, 128), BF),
        in_specs=[VM],
        out_specs=VM,
        compiler_params=PARAMS,
    )(parts)


def after_layers(parts):
    return pl.pallas_call(
        layer_kernel,
        out_shape=shape((32, 40, 128), BF),
        in_specs=[VM],
        out_specs=VM,
        compiler_params=PARAMS,
    )(parts)


def last(index, total, recv1, recv2, hidden, tiles, w1s, w1n, bias, w2s_t, w2n_t):
    shapes = (
        shape((172, 512), BF),
        shape((128, 256), F32),
        shape((128, 256), F32),
        shape((1, 256), F32),
        shape((172, 256), F32),
        shape((172, 256), F32),
    )
    return pl.pallas_call(
        last_kernel,
        out_shape=shapes,
        in_specs=[VM] * 11,
        out_specs=(pl.BlockSpec(memory_space=pltpu.HBM),) * 6,
        scratch_shapes=[pltpu.VMEM(one.shape, one.dtype) for one in shapes]
        + [pltpu.VMEM((6, 128, 256), BF), pltpu.VMEM((512, 256), BF), pltpu.SemaphoreType.DMA((6,)), pltpu.SMEM((3, 1, 4), jnp.int32), pltpu.SemaphoreType.DMA],
        compiler_params=PARAMS,
    )(index, total, recv1, recv2, hidden, tiles, w1s, w1n, bias, w2s_t, w2n_t)


def exchange(values, axes):
    return lax.all_to_all(values, axes, split_axis=0, concat_axis=0, tiled=True)


def shards(
    features,
    send_rows,
    send_counts,
    tile_index,
    tile_weight,
    first_layer_self_weight,
    first_layer_neighbour_weight,
    layer1_bias,
    layer2_self,
    layer2_neigh,
    grad_logits,
):
    feat = features.reshape(512, 128)
    rows = jnp.swapaxes(send_rows.reshape(128, 2), 0, 1)
    counts = send_counts.reshape(1, 128)
    index = jnp.transpose(tile_index, (0, 3, 1, 2)).reshape(3, 1, 4)
    tiles = tile_weight.reshape(12, 128, 128)
    grad_t = jnp.swapaxes(grad_logits.reshape(512, 172), 0, 1)
    w2s_t = jnp.swapaxes(layer2_self, 0, 1)
    w2n_t = jnp.swapaxes(layer2_neigh, 0, 1)
    bias = layer1_bias.reshape(1, 256)

    send1, pick, pick_out, own_t, feat, grad_t, tiles, w1s, w1n, bias, w2s_t, w2n_t, index = before(
        rows, counts, feat, grad_t, tiles,
        first_layer_self_weight, first_layer_neighbour_weight, bias, w2s_t, w2n_t, index,
    )
    recv1 = exchange(send1.reshape(128, 2, 384), WIDE).reshape(256, 384)
    hidden, parts = middle(
        index, recv1, feat, tiles, pick, pick_out, own_t, grad_t,
        w1s, w1n, bias, w2s_t, w2n_t,
    )
    recv2 = exchange(after_plane(exchange(parts, PLANE)), "z")
    total = exchange(after_layers(recv2), PLANE)
    logits_t, self1, neigh1, bias1, self2_t, neigh2_t = last(
        index, total.reshape(1280, 128), recv1, recv2, hidden, tiles, w1s, w1n, bias, w2s_t, w2n_t,
    )
    logits = jnp.swapaxes(logits_t, 0, 1).reshape(1, 1, 512, 172)
    return (
        logits,
        self1,
        neigh1,
        bias1.reshape(256),
        jnp.swapaxes(self2_t, 0, 1),
        jnp.swapaxes(neigh2_t, 0, 1),
    )


def solution(mesh):
    fine = Mesh(mesh.devices.reshape(16, 4, 2, 4), ("z", "x", "core", "y"))
    return jax.shard_map(
        shards,
        mesh=fine,
        in_specs=(
            P(WIDE, "y", None, None),
            P(WIDE, "y", None, None),
            P(WIDE, "y", None),
            P(WIDE, "y", None, None),
            P(WIDE, "y", None, None, None, None),
            P(),
            P(),
            P(),
            P(),
            P(),
            P(WIDE, "y", None, None),
        ),
        out_specs=(P(WIDE, "y", None, None), P(), P(), P(), P(), P()),
        check_vma=False,
    )
```

```python
import jax
import jax.numpy as jnp
from jax import lax
from jax.experimental import pallas as pl
from jax.experimental.pallas import tpu as pltpu
from jax.sharding import Mesh, PartitionSpec as P

BF = jnp.bfloat16
F32 = jnp.float32
PLANE = ("x", "core", "y")
WIDE = ("z", "x", "core")
VM = pl.BlockSpec(memory_space=pltpu.VMEM)
SM = pl.BlockSpec(memory_space=pltpu.SMEM)
PARAMS = pltpu.CompilerParams(vmem_limit_bytes=32 * 1024 * 1024)


def dot(a, b):
    return jnp.dot(a, b, preferred_element_type=F32)


def dot_nt(a, b):
    return lax.dot_general(a, b, (((1,), (1,)), ((), ())), preferred_element_type=F32)


def dot_tn(a, b):
    return lax.dot_general(a, b, (((0,), (0,)), ((), ())), preferred_element_type=F32)


def place():
    return lax.axis_index("y")


def before_kernel(*refs):
    rows_in, counts_in = refs[0:2]
    send, pick, pick_out, own_t = refs[11:15]
    feat, grad_t, tiles = refs[15:18]
    rows, counts, index, acc, padded, sems = refs[24:30]
    pairs = [(rows_in, rows), (counts_in, counts)] + list(zip(refs[2:11], refs[15:24])) + [(refs[10], index)]
    copies = [pltpu.make_async_copy(a, b, sems.at[i]) for i, (a, b) in enumerate(pairs)]
    for copy in copies:
        copy.start()
    acc[...] = jnp.zeros_like(acc)
    padded[...] = jnp.zeros_like(padded)
    i = lax.broadcasted_iota(jnp.int32, (256, 256), 0)
    j = lax.broadcasted_iota(jnp.int32, (256, 256), 1)
    orders = (((i & 1) * 128 + (i >> 1), pick), (((i >> 4) & 1) * 128 + (i & 15) * 8 + (i >> 5), pick_out))
    copies[0].wait()
    copies[1].wait()
    slot = lax.broadcasted_iota(jnp.int32, (2, 128), 0)
    wanted = jnp.where(slot < counts[...], rows[...], 512)
    by_slot = jnp.concatenate([wanted[0:1, :], wanted[1:2, :]], axis=1)
    wide_rows = jnp.broadcast_to(by_slot, (128, 256))
    half = wide_rows // 2
    low = wide_rows - half * 2
    half = half.astype(F32).astype(BF)
    low = low.astype(F32).astype(BF)
    lane = lax.broadcasted_iota(jnp.int32, (256, 128), 1).astype(F32)
    for place_of, target in orders:
        perm = jnp.where(j == place_of, 1.0, 0.0).astype(BF)
        column = 2.0 * dot_nt(perm, half) + dot_nt(perm, low)
        if target is pick:
            live = jnp.where(column < 512.0, 1.0, 0.0)
        for c in range(4):
            target[:, c * 128 : (c + 1) * 128] = jnp.where(column == lane + 128.0 * c, 1.0, 0.0).astype(BF)
    copies[2].wait()
    send[:, 0:128] = dot(pick[...], feat[...]).astype(BF)
    copies[3].wait()
    padded[0:172, :] = grad_t[...]
    copies[4].wait()
    copies[11].wait()
    for b in range(4):
        part = padded[:, b * 128 : (b + 1) * 128]
        for k in range(3):
            e = index[k, 0, b]
            acc[e] += dot(part, tiles[b * 3 + k])
    for b in range(4):
        own_t[:, b * 128 : (b + 1) * 128] = acc[b]
    for b in range(2):
        rows_of = slice(b * 128, (b + 1) * 128)
        back = acc[4 + b].T
        tail = jnp.where(lane[rows_of, :] == 44.0, live[rows_of, :], back[:, 128:256])
        send[rows_of, 128:256] = back[:, 0:128].astype(BF)
        send[rows_of, 256:384] = tail.astype(BF)
    for copy in copies[5:11]:
        copy.wait()


def gather_tiles(index, tiles, ext, b):
    total = dot(tiles[b * 3], ext[index[0, 0, b]])
    total += dot(tiles[b * 3 + 1], ext[index[1, 0, b]])
    total += dot(tiles[b * 3 + 2], ext[index[2, 0, b]])
    return total.astype(BF)


def middle_kernel(
    index_in, recv, feat, tiles, pick, pick_out, own_t, grad_t, w1s, w1n, bias, w2s_t, w2n_t,
    hidden, out, ext, both, padded, wide_w, index, sem,
):
    copy = pltpu.make_async_copy(index_in, index, sem)
    copy.start()
    recv = recv[...].reshape(256, 384)
    for b in range(4):
        ext[b] = feat[b * 128 : (b + 1) * 128, :]
    for b in range(2):
        ext[4 + b] = recv[b * 128 : (b + 1) * 128, 0:128]
    both[:, 0:128] = feat[...]
    wide_w[...] = jnp.zeros_like(wide_w)
    padded[...] = jnp.zeros_like(padded)
    padded[0:172, :] = grad_t[...]
    wide_w[0:172, :] = w2s_t[...]
    wide_w[256 : 256 + 172, :] = w2n_t[...]
    returned_t = recv[:, 128:384].astype(F32).T.astype(BF)
    back_t = own_t[...] + dot(returned_t, pick[...])
    copy.wait()
    upper_t = back_t.astype(BF)
    grad = padded[...]
    grad_hidden = dot_tn(jnp.concatenate([grad, upper_t], axis=0), wide_w[...])
    for b in range(4):
        both[b * 128 : (b + 1) * 128, 128:256] = gather_tiles(index, tiles, ext, b)
    picked = dot(pick_out[...], both[:, 128:256]).astype(BF)
    y = place()
    for p in range(8):
        out[p * 4 + y, 0:32, :] = picked[p * 32 : (p + 1) * 32, :]
    pre = dot(both[:, 0:128], w1s[...]) + dot(both[:, 128:256], w1n[...]) + bias[...]
    hid = jnp.maximum(pre, 0.0).astype(BF)
    hidden[...] = hid
    grad_pre = jnp.where(pre > 0, grad_hidden, 0.0).astype(BF)
    first = dot(both[...].astype(F32).T.astype(BF), grad_pre)
    bias_sum = jnp.sum(grad_pre.astype(F32), axis=0, keepdims=True)
    self2 = dot(grad, hid)
    neigh2 = dot(upper_t, hid)
    row = lax.broadcasted_iota(jnp.int32, (176, 256), 0)
    self2 = jnp.where(row == 172, bias_sum, self2[0:176, :])
    neigh2 = neigh2[0:176, :]
    rest = jnp.concatenate([self2, neigh2, jnp.zeros((32, 256), F32)], axis=0)
    grads = jnp.concatenate([first, rest], axis=0).astype(BF)
    for p in range(32):
        out[p, 32:72, :] = grads[(p % 16) * 40 : (p % 16) * 40 + 40, (p // 16) * 128 : (p // 16) * 128 + 128]


def plane_kernel(parts, out):
    total = parts[0, 32:72, :].astype(F32)
    for p in range(1, 32):
        total += parts[p, 32:72, :].astype(F32)
    total = total.astype(BF)
    y = place()
    i = lax.broadcasted_iota(jnp.int32, (256, 256), 0)
    j = lax.broadcasted_iota(jnp.int32, (256, 256), 1)
    place_of = ((i >> 1) & 7) * 32 + (i & 1) * 16 + (i >> 4)
    rows = jnp.concatenate([parts[p * 4 + y, 0:32, :] for p in range(8)], axis=0)
    rows = dot(jnp.where(j == place_of, 1.0, 0.0).astype(BF), rows).astype(BF)
    for z in range(16):
        out[z, 0:16, :] = rows[z * 16 : (z + 1) * 16, :]
        out[z, 16:56, :] = total


def layer_kernel(parts, out):
    total = parts[0, 16:56, :].astype(F32)
    for p in range(1, 16):
        total += parts[p, 16:56, :].astype(F32)
    total = total.astype(BF)
    for p in range(32):
        out[p] = total


def last_kernel(
    index_in, total, recv1, recv2, hidden, tiles, w1s, w1n, bias, w2s_t, w2n_t,
    logits_out, self1_out, neigh1_out, bias_out, self2_out, neigh2_out,
    logits, self1, neigh1, bias1, self2_t, neigh2_t, ext, agg, sems, index, index_sem,
):
    copies = []
    fetch = pltpu.make_async_copy(index_in, index, index_sem)
    fetch.start()
    recv1 = recv1[...].reshape(256, 384)

    def leave(value, target):
        copies.append(pltpu.make_async_copy(value, target, sems.at[len(copies)]))
        copies[-1].start()

    def both(first, rows):
        halves = [total[base + first : base + first + rows, :].astype(F32) for base in (0, 640)]
        return jnp.concatenate(halves, axis=1)

    self1[...] = both(0, 128)
    neigh1[...] = both(128, 128)
    value = both(256, 176)
    self2_t[...] = value[0:172, :]
    bias1[...] = value[172:173, :]
    neigh2_t[...] = both(432, 176)[0:172, :]
    far = jnp.concatenate([recv2[z, 0:16, :] for z in range(16)], axis=0)
    pre = dot(recv1[:, 0:128], w1s[...]) + dot(far, w1n[...]) + bias[...]
    i = lax.broadcasted_iota(jnp.int32, (128, 256), 0)
    live = dot(recv1[:, 256:384], jnp.where(i == 44, 1.0, 0.0).astype(BF))
    far = jnp.where(live > 0.5, jnp.maximum(pre, 0.0), 0.0).astype(BF)
    for b in range(4):
        ext[b] = hidden[b * 128 : (b + 1) * 128, :]
    for b in range(2):
        ext[4 + b] = far[b * 128 : (b + 1) * 128, :]
    scores = dot_nt(w2s_t[...], hidden[...])
    fetch.wait()
    leave(self1, self1_out)
    leave(neigh1, neigh1_out)
    leave(self2_t, self2_out)
    leave(bias1, bias_out)
    leave(neigh2_t, neigh2_out)
    for b in range(4):
        agg[b * 128 : (b + 1) * 128, :] = gather_tiles(index, tiles, ext, b)
    scores += dot_nt(w2n_t[...], agg[...])
    logits[...] = scores.astype(BF)
    leave(logits, logits_out)
    for copy in copies:
        copy.wait()


def shape(dims, dtype):
    return jax.ShapeDtypeStruct(dims, dtype)


def before(rows, counts, *kept):
    here = [pltpu.with_memory_space_constraint(value, pltpu.HBM) for value in (rows, counts) + kept]
    return pl.pallas_call(
        before_kernel,
        out_shape=(shape((256, 384), BF), shape((256, 512), BF), shape((256, 512), BF), shape((256, 512), F32))
        + tuple(shape(value.shape, value.dtype) for value in kept),
        in_specs=[pl.BlockSpec(memory_space=pltpu.HBM)] * 11,
        out_specs=(VM,) * 13,
        scratch_shapes=[
            pltpu.VMEM((2, 128), jnp.int32),
            pltpu.VMEM((1, 128), jnp.int32),
            pltpu.SMEM((3, 1, 4), jnp.int32),
            pltpu.VMEM((6, 256, 128), F32),
            pltpu.VMEM((256, 512), BF),
            pltpu.SemaphoreType.DMA((12,)),
        ],
        compiler_params=PARAMS,
    )(*here)


def middle(index, recv, feat, tiles, pick, pick_out, own_t, grad_t, w1s, w1n, bias, w2s_t, w2n_t):
    return pl.pallas_call(
        middle_kernel,
        out_shape=(shape((512, 256), BF), shape((32, 72, 128), BF)),
        in_specs=[VM] * 13,
        out_specs=(VM, VM),
        scratch_shapes=[
            pltpu.VMEM((6, 128, 128), BF),
            pltpu.VMEM((512, 256), BF),
            pltpu.VMEM((256, 512), BF),
            pltpu.VMEM((512, 256), BF),
            pltpu.SMEM((3, 1, 4), jnp.int32),
            pltpu.SemaphoreType.DMA,
        ],
        compiler_params=PARAMS,
    )(index, recv, feat, tiles, pick, pick_out, own_t, grad_t, w1s, w1n, bias, w2s_t, w2n_t)


def after_plane(parts):
    return pl.pallas_call(
        plane_kernel,
        out_shape=shape((16, 56, 128), BF),
        in_specs=[VM],
        out_specs=VM,
        compiler_params=PARAMS,
    )(parts)


def after_layers(parts):
    return pl.pallas_call(
        layer_kernel,
        out_shape=shape((32, 40, 128), BF),
        in_specs=[VM],
        out_specs=VM,
        compiler_params=PARAMS,
    )(parts)


def last(index, total, recv1, recv2, hidden, tiles, w1s, w1n, bias, w2s_t, w2n_t):
    shapes = (
        shape((172, 512), BF),
        shape((128, 256), F32),
        shape((128, 256), F32),
        shape((1, 256), F32),
        shape((172, 256), F32),
        shape((172, 256), F32),
    )
    return pl.pallas_call(
        last_kernel,
        out_shape=shapes,
        in_specs=[VM] * 11,
        out_specs=(pl.BlockSpec(memory_space=pltpu.HBM),) * 6,
        scratch_shapes=[pltpu.VMEM(one.shape, one.dtype) for one in shapes]
        + [pltpu.VMEM((6, 128, 256), BF), pltpu.VMEM((512, 256), BF), pltpu.SemaphoreType.DMA((6,)), pltpu.SMEM((3, 1, 4), jnp.int32), pltpu.SemaphoreType.DMA],
        compiler_params=PARAMS,
    )(index, total, recv1, recv2, hidden, tiles, w1s, w1n, bias, w2s_t, w2n_t)


def exchange(values, axes):
    return lax.all_to_all(values, axes, split_axis=0, concat_axis=0, tiled=True)


def shards(
    features,
    send_rows,
    send_counts,
    tile_index,
    tile_weight,
    first_layer_self_weight,
    first_layer_neighbour_weight,
    layer1_bias,
    layer2_self,
    layer2_neigh,
    grad_logits,
):
    feat = features.reshape(512, 128)
    rows = jnp.swapaxes(send_rows.reshape(128, 2), 0, 1)
    counts = send_counts.reshape(1, 128)
    index = jnp.transpose(tile_index, (0, 3, 1, 2)).reshape(3, 1, 4)
    tiles = tile_weight.reshape(12, 128, 128)
    grad_t = jnp.swapaxes(grad_logits.reshape(512, 172), 0, 1)
    w2s_t = jnp.swapaxes(layer2_self, 0, 1)
    w2n_t = jnp.swapaxes(layer2_neigh, 0, 1)
    bias = layer1_bias.reshape(1, 256)

    send1, pick, pick_out, own_t, feat, grad_t, tiles, w1s, w1n, bias, w2s_t, w2n_t, index = before(
        rows, counts, feat, grad_t, tiles,
        first_layer_self_weight, first_layer_neighbour_weight, bias, w2s_t, w2n_t, index,
    )
    recv1 = exchange(send1.reshape(128, 2, 384), WIDE)
    hidden, parts = middle(
        index, recv1, feat, tiles, pick, pick_out, own_t, grad_t,
        w1s, w1n, bias, w2s_t, w2n_t,
    )
    recv2 = exchange(after_plane(exchange(parts, PLANE)), "z")
    total = exchange(after_layers(recv2), PLANE)
    logits_t, self1, neigh1, bias1, self2_t, neigh2_t = last(
        index, total.reshape(1280, 128), recv1, recv2, hidden, tiles, w1s, w1n, bias, w2s_t, w2n_t,
    )
    logits = jnp.swapaxes(logits_t, 0, 1).reshape(1, 1, 512, 172)
    return (
        logits,
        self1,
        neigh1,
        bias1.reshape(256),
        jnp.swapaxes(self2_t, 0, 1),
        jnp.swapaxes(neigh2_t, 0, 1),
    )


def solution(mesh):
    fine = Mesh(mesh.devices.reshape(16, 4, 2, 4), ("z", "x", "core", "y"))
    return jax.shard_map(
        shards,
        mesh=fine,
        in_specs=(
            P(WIDE, "y", None, None),
            P(WIDE, "y", None, None),
            P(WIDE, "y", None),
            P(WIDE, "y", None, None),
            P(WIDE, "y", None, None, None, None),
            P(),
            P(),
            P(),
            P(),
            P(),
            P(WIDE, "y", None, None),
        ),
        out_specs=(P(WIDE, "y", None, None), P(), P(), P(), P(), P()),
        check_vma=False,
    )
```

```python
import jax
import jax.numpy as jnp
from jax import lax
from jax.experimental import pallas as pl
from jax.experimental.pallas import tpu as pltpu
from jax.sharding import Mesh, PartitionSpec as P

BF = jnp.bfloat16
F32 = jnp.float32
PLANE = ("x", "core", "y")
WIDE = ("z", "x", "core")
VM = pl.BlockSpec(memory_space=pltpu.VMEM)
SM = pl.BlockSpec(memory_space=pltpu.SMEM)
PARAMS = pltpu.CompilerParams(vmem_limit_bytes=32 * 1024 * 1024)


def dot(a, b):
    return jnp.dot(a, b, preferred_element_type=F32)


def dot_nt(a, b):
    return lax.dot_general(a, b, (((1,), (1,)), ((), ())), preferred_element_type=F32)


def dot_tn(a, b):
    return lax.dot_general(a, b, (((0,), (0,)), ((), ())), preferred_element_type=F32)


def place():
    return lax.axis_index("y")


def before_kernel(*refs):
    rows_in, counts_in = refs[0:2]
    send, pick, pick_out, own_t = refs[11:15]
    feat, grad_t, tiles = refs[15:18]
    rows, counts, index, acc, padded, sems = refs[24:30]
    pairs = [(rows_in, rows), (counts_in, counts)] + list(zip(refs[2:11], refs[15:24])) + [(refs[10], index)]
    copies = [pltpu.make_async_copy(a, b, sems.at[i]) for i, (a, b) in enumerate(pairs)]
    for copy in copies:
        copy.start()
    acc[...] = jnp.zeros_like(acc)
    padded[...] = jnp.zeros_like(padded)
    i = lax.broadcasted_iota(jnp.int32, (256, 256), 0)
    j = lax.broadcasted_iota(jnp.int32, (256, 256), 1)
    orders = (((i & 1) * 128 + (i >> 1), pick), (((i >> 4) & 1) * 128 + (i & 15) * 8 + (i >> 5), pick_out))
    copies[0].wait()
    copies[1].wait()
    slot = lax.broadcasted_iota(jnp.int32, (2, 128), 0)
    wanted = jnp.where(slot < counts[...], rows[...], 512)
    by_slot = jnp.concatenate([wanted[0:1, :], wanted[1:2, :]], axis=1)
    wide_rows = jnp.broadcast_to(by_slot, (128, 256))
    half = wide_rows // 2
    low = wide_rows - half * 2
    half = half.astype(F32).astype(BF)
    low = low.astype(F32).astype(BF)
    lane = lax.broadcasted_iota(jnp.int32, (256, 128), 1).astype(F32)
    for place_of, target in orders:
        perm = jnp.where(j == place_of, 1.0, 0.0).astype(BF)
        column = 2.0 * dot_nt(perm, half) + dot_nt(perm, low)
        if target is pick:
            live = jnp.where(column < 512.0, 1.0, 0.0)
        for c in range(4):
            target[:, c * 128 : (c + 1) * 128] = jnp.where(column == lane + 128.0 * c, 1.0, 0.0).astype(BF)
    copies[2].wait()
    send[:, 0:128] = dot(pick[...], feat[...]).astype(BF)
    copies[3].wait()
    padded[0:172, :] = grad_t[...]
    copies[4].wait()
    copies[11].wait()
    for b in range(4):
        part = padded[:, b * 128 : (b + 1) * 128]
        for k in range(3):
            e = index[k, 0, b]
            acc[e] += dot(part, tiles[b * 3 + k])
    for b in range(4):
        own_t[:, b * 128 : (b + 1) * 128] = acc[b]
    for b in range(2):
        rows_of = slice(b * 128, (b + 1) * 128)
        back = acc[4 + b].T
        tail = jnp.where(lane[rows_of, :] == 44.0, live[rows_of, :], back[:, 128:256])
        send[rows_of, 128:256] = back[:, 0:128].astype(BF)
        send[rows_of, 256:384] = tail.astype(BF)
    for copy in copies[5:11]:
        copy.wait()


def gather_tiles(index, tiles, ext, b):
    total = dot(tiles[b * 3], ext[b])
    total += dot(tiles[b * 3 + 1], ext[index[1, 0, b]])
    total += dot(tiles[b * 3 + 2], ext[index[2, 0, b]])
    return total.astype(BF)


def middle_kernel(
    index_in, recv, feat, tiles, pick, pick_out, own_t, grad_t, w1s, w1n, bias, w2s_t, w2n_t,
    hidden, out, ext, both, padded, wide_w, index, sem,
):
    copy = pltpu.make_async_copy(index_in, index, sem)
    copy.start()
    for b in range(4):
        ext[b] = feat[b * 128 : (b + 1) * 128, :]
    for b in range(2):
        ext[4 + b] = recv[b * 128 : (b + 1) * 128, 0:128]
    both[:, 0:128] = feat[...]
    wide_w[...] = jnp.zeros_like(wide_w)
    padded[...] = jnp.zeros_like(padded)
    padded[0:172, :] = grad_t[...]
    wide_w[0:172, :] = w2s_t[...]
    wide_w[256 : 256 + 172, :] = w2n_t[...]
    returned_t = recv[:, 128:384].astype(F32).T.astype(BF)
    back_t = own_t[...] + dot(returned_t, pick[...])
    copy.wait()
    upper_t = back_t.astype(BF)
    grad = padded[...]
    grad_hidden = dot_tn(jnp.concatenate([grad, upper_t], axis=0), wide_w[...])
    for b in range(4):
        both[b * 128 : (b + 1) * 128, 128:256] = gather_tiles(index, tiles, ext, b)
    picked = dot(pick_out[...], both[:, 128:256]).astype(BF)
    y = place()
    for p in range(8):
        out[p * 4 + y, 0:32, :] = picked[p * 32 : (p + 1) * 32, :]
    pre = dot(both[:, 0:128], w1s[...]) + dot(both[:, 128:256], w1n[...]) + bias[...]
    hid = jnp.maximum(pre, 0.0).astype(BF)
    hidden[...] = hid
    grad_pre = jnp.where(pre > 0, grad_hidden, 0.0).astype(BF)
    first = dot(both[...].astype(F32).T.astype(BF), grad_pre)
    bias_sum = jnp.sum(grad_pre.astype(F32), axis=0, keepdims=True)
    self2 = dot(grad, hid)
    neigh2 = dot(upper_t, hid)
    row = lax.broadcasted_iota(jnp.int32, (176, 256), 0)
    self2 = jnp.where(row == 172, bias_sum, self2[0:176, :])
    neigh2 = neigh2[0:176, :]
    rest = jnp.concatenate([self2, neigh2, jnp.zeros((32, 256), F32)], axis=0)
    grads = jnp.concatenate([first, rest], axis=0).astype(BF)
    for p in range(32):
        out[p, 32:72, :] = grads[(p % 16) * 40 : (p % 16) * 40 + 40, (p // 16) * 128 : (p // 16) * 128 + 128]


def plane_kernel(parts, out):
    total = parts[0, 32:72, :].astype(F32)
    for p in range(1, 32):
        total += parts[p, 32:72, :].astype(F32)
    total = total.astype(BF)
    y = place()
    i = lax.broadcasted_iota(jnp.int32, (256, 256), 0)
    j = lax.broadcasted_iota(jnp.int32, (256, 256), 1)
    place_of = ((i >> 1) & 7) * 32 + (i & 1) * 16 + (i >> 4)
    rows = jnp.concatenate([parts[p * 4 + y, 0:32, :] for p in range(8)], axis=0)
    rows = dot(jnp.where(j == place_of, 1.0, 0.0).astype(BF), rows).astype(BF)
    for z in range(16):
        out[z, 0:16, :] = rows[z * 16 : (z + 1) * 16, :]
        out[z, 16:56, :] = total


def layer_kernel(parts, out):
    total = parts[0, 16:56, :].astype(F32)
    for p in range(1, 16):
        total += parts[p, 16:56, :].astype(F32)
    total = total.astype(BF)
    for p in range(32):
        out[p] = total


def last_kernel(
    index_in, total, recv1, recv2, hidden, tiles, w1s, w1n, bias, w2s_t, w2n_t,
    logits_out, self1_out, neigh1_out, bias_out, self2_out, neigh2_out,
    logits, self1, neigh1, bias1, self2_t, neigh2_t, ext, agg, sems, index, index_sem,
):
    copies = []
    fetch = pltpu.make_async_copy(index_in, index, index_sem)
    fetch.start()

    def leave(value, target):
        copies.append(pltpu.make_async_copy(value, target, sems.at[len(copies)]))
        copies[-1].start()

    def both(first, rows):
        halves = [total[base + first : base + first + rows, :].astype(F32) for base in (0, 640)]
        return jnp.concatenate(halves, axis=1)

    self1[...] = both(0, 128)
    leave(self1, self1_out)
    neigh1[...] = both(128, 128)
    leave(neigh1, neigh1_out)
    value = both(256, 176)
    self2_t[...] = value[0:172, :]
    leave(self2_t, self2_out)
    bias1[...] = value[172:173, :]
    leave(bias1, bias_out)
    neigh2_t[...] = both(432, 176)[0:172, :]
    leave(neigh2_t, neigh2_out)
    far = jnp.concatenate([recv2[z, 0:16, :] for z in range(16)], axis=0)
    pre = dot(recv1[:, 0:128], w1s[...]) + dot(far, w1n[...]) + bias[...]
    i = lax.broadcasted_iota(jnp.int32, (128, 256), 0)
    live = dot(recv1[:, 256:384], jnp.where(i == 44, 1.0, 0.0).astype(BF))
    far = jnp.where(live > 0.5, jnp.maximum(pre, 0.0), 0.0).astype(BF)
    for b in range(4):
        ext[b] = hidden[b * 128 : (b + 1) * 128, :]
    for b in range(2):
        ext[4 + b] = far[b * 128 : (b + 1) * 128, :]
    scores = dot_nt(w2s_t[...], hidden[...])
    fetch.wait()
    for b in range(4):
        agg[b * 128 : (b + 1) * 128, :] = gather_tiles(index, tiles, ext, b)
    scores += dot_nt(w2n_t[...], agg[...])
    logits[...] = scores.astype(BF)
    leave(logits, logits_out)
    for copy in copies:
        copy.wait()


def shape(dims, dtype):
    return jax.ShapeDtypeStruct(dims, dtype)


def before(rows, counts, *kept):
    here = [pltpu.with_memory_space_constraint(value, pltpu.HBM) for value in (rows, counts) + kept]
    return pl.pallas_call(
        before_kernel,
        out_shape=(shape((256, 384), BF), shape((256, 512), BF), shape((256, 512), BF), shape((256, 512), F32))
        + tuple(shape(value.shape, value.dtype) for value in kept),
        in_specs=[pl.BlockSpec(memory_space=pltpu.HBM)] * 11,
        out_specs=(VM,) * 13,
        scratch_shapes=[
            pltpu.VMEM((2, 128), jnp.int32),
            pltpu.VMEM((1, 128), jnp.int32),
            pltpu.SMEM((3, 1, 4), jnp.int32),
            pltpu.VMEM((6, 256, 128), F32),
            pltpu.VMEM((256, 512), BF),
            pltpu.SemaphoreType.DMA((12,)),
        ],
        compiler_params=PARAMS,
    )(*here)


def middle(index, recv, feat, tiles, pick, pick_out, own_t, grad_t, w1s, w1n, bias, w2s_t, w2n_t):
    return pl.pallas_call(
        middle_kernel,
        out_shape=(shape((512, 256), BF), shape((32, 72, 128), BF)),
        in_specs=[VM] * 13,
        out_specs=(VM, VM),
        scratch_shapes=[
            pltpu.VMEM((6, 128, 128), BF),
            pltpu.VMEM((512, 256), BF),
            pltpu.VMEM((256, 512), BF),
            pltpu.VMEM((512, 256), BF),
            pltpu.SMEM((3, 1, 4), jnp.int32),
            pltpu.SemaphoreType.DMA,
        ],
        compiler_params=PARAMS,
    )(index, recv, feat, tiles, pick, pick_out, own_t, grad_t, w1s, w1n, bias, w2s_t, w2n_t)


def after_plane(parts):
    return pl.pallas_call(
        plane_kernel,
        out_shape=shape((16, 56, 128), BF),
        in_specs=[VM],
        out_specs=VM,
        compiler_params=PARAMS,
    )(parts)


def after_layers(parts):
    return pl.pallas_call(
        layer_kernel,
        out_shape=shape((32, 40, 128), BF),
        in_specs=[VM],
        out_specs=VM,
        compiler_params=PARAMS,
    )(parts)


def last(index, total, recv1, recv2, hidden, tiles, w1s, w1n, bias, w2s_t, w2n_t):
    shapes = (
        shape((172, 512), BF),
        shape((128, 256), F32),
        shape((128, 256), F32),
        shape((1, 256), F32),
        shape((172, 256), F32),
        shape((172, 256), F32),
    )
    return pl.pallas_call(
        last_kernel,
        out_shape=shapes,
        in_specs=[VM] * 11,
        out_specs=(pl.BlockSpec(memory_space=pltpu.HBM),) * 6,
        scratch_shapes=[pltpu.VMEM(one.shape, one.dtype) for one in shapes]
        + [pltpu.VMEM((6, 128, 256), BF), pltpu.VMEM((512, 256), BF), pltpu.SemaphoreType.DMA((6,)), pltpu.SMEM((3, 1, 4), jnp.int32), pltpu.SemaphoreType.DMA],
        compiler_params=PARAMS,
    )(index, total, recv1, recv2, hidden, tiles, w1s, w1n, bias, w2s_t, w2n_t)


def exchange(values, axes):
    return lax.all_to_all(values, axes, split_axis=0, concat_axis=0, tiled=True)


def shards(
    features,
    send_rows,
    send_counts,
    tile_index,
    tile_weight,
    first_layer_self_weight,
    first_layer_neighbour_weight,
    layer1_bias,
    layer2_self,
    layer2_neigh,
    grad_logits,
):
    feat = features.reshape(512, 128)
    rows = jnp.swapaxes(send_rows.reshape(128, 2), 0, 1)
    counts = send_counts.reshape(1, 128)
    index = jnp.transpose(tile_index, (0, 3, 1, 2)).reshape(3, 1, 4)
    tiles = tile_weight.reshape(12, 128, 128)
    grad_t = jnp.swapaxes(grad_logits.reshape(512, 172), 0, 1)
    w2s_t = jnp.swapaxes(layer2_self, 0, 1)
    w2n_t = jnp.swapaxes(layer2_neigh, 0, 1)
    bias = layer1_bias.reshape(1, 256)

    send1, pick, pick_out, own_t, feat, grad_t, tiles, w1s, w1n, bias, w2s_t, w2n_t, index = before(
        rows, counts, feat, grad_t, tiles,
        first_layer_self_weight, first_layer_neighbour_weight, bias, w2s_t, w2n_t, index,
    )
    recv1 = exchange(send1.reshape(128, 2, 384), WIDE).reshape(256, 384)
    hidden, parts = middle(
        index, recv1, feat, tiles, pick, pick_out, own_t, grad_t,
        w1s, w1n, bias, w2s_t, w2n_t,
    )
    recv2 = exchange(after_plane(exchange(parts, PLANE)), "z")
    total = exchange(after_layers(recv2), PLANE)
    logits_t, self1, neigh1, bias1, self2_t, neigh2_t = last(
        index, total.reshape(1280, 128), recv1, recv2, hidden, tiles, w1s, w1n, bias, w2s_t, w2n_t,
    )
    logits = jnp.swapaxes(logits_t, 0, 1).reshape(1, 1, 512, 172)
    return (
        logits,
        self1,
        neigh1,
        bias1.reshape(256),
        jnp.swapaxes(self2_t, 0, 1),
        jnp.swapaxes(neigh2_t, 0, 1),
    )


def solution(mesh):
    fine = Mesh(mesh.devices.reshape(16, 4, 2, 4), ("z", "x", "core", "y"))
    return jax.shard_map(
        shards,
        mesh=fine,
        in_specs=(
            P(WIDE, "y", None, None),
            P(WIDE, "y", None, None),
            P(WIDE, "y", None),
            P(WIDE, "y", None, None),
            P(WIDE, "y", None, None, None, None),
            P(),
            P(),
            P(),
            P(),
            P(),
            P(WIDE, "y", None, None),
        ),
        out_specs=(P(WIDE, "y", None, None), P(), P(), P(), P(), P()),
        check_vma=False,
    )
```
